32 devices in a mesh: seq: 8 (over z, y), head: 4 (over x, core).
Axes of the slice: x: 2, y: 2, z: 4, core: 2. Of those that a mesh axis runs over, the one named last changes fastest.
Arguments:
- queries: bfloat16 [4096, 2048], P(('seq', 'head')), may hold values from -27 to 27
- key_vectors: bfloat16 [4096, 2048], P(('seq', 'head')), may hold values from -6 to 6
- value_vectors: bfloat16 [4096, 2048], P(('seq', 'head')), may hold values from -6 to 6
- grad_output: bfloat16 [4096, 2048], P(('seq', 'head')), may hold values from -6 to 6
Outputs:
- grad_queries: bfloat16 [4096, 2048], P(('seq', 'head'))
- grad_keys: bfloat16 [4096, 2048], P(('seq', 'head'))
- grad_values: bfloat16 [4096, 2048], P(('seq', 'head'))
The draws below stay inside these ranges and needn't reach their ends.
All inputs are finite; a program needn't handle non-finite values.
Results may differ from the reference program's by a relative error of at most 0.009.
Values may be sent and summed in bfloat16 or wider, within the bound.
No kernel may reach another device: no remote copies, remote signals or barrier semaphores. Data moves between devices by JAX's collectives and lax.ppermute only.
A program may use at most 64 MiB of HBM per device.

```python
import jax
import jax.numpy as jnp
from jax import lax

HEADS = 16
HEAD_DIM = 128
D = 2048
WINDOW = 512
TOKENS = 4096


def drawn_pair(key):
    key_query = jax.random.fold_in(key, 11)
    key_key = jax.random.fold_in(key, 12)
    shape = (TOKENS, D)
    query_out = jnp.clip(jax.random.normal(key_query, shape, jnp.float32), -6.0, 6.0)
    key_out = jnp.clip(jax.random.normal(key_key, shape, jnp.float32), -6.0, 6.0)
    return (query_out, key_out)


def draw_queries(key, part):
    return drawn_pair(key)[0].astype(jnp.bfloat16)


def draw_key_vectors(key, part):
    return drawn_pair(key)[1].astype(jnp.bfloat16)


def levels(stream_key, extent, pieces, least, high):
    level = 1.0
    for position, shards_of in pieces:
        steps = jax.random.uniform(jax.random.fold_in(jax.random.fold_in(stream_key, 6), position), (shards_of,), jnp.float32, least / len(pieces), high / len(pieces))
        level = level * jnp.repeat(jnp.exp(steps), extent[position] // shards_of).reshape((-1,) + (1,) * (len(extent) - 1 - position))
    return level


def centred(rng, dims, scale, limit, cuts=(), kind=jnp.bfloat16):
    result = scale * jax.random.normal(rng, dims, jnp.float32)
    if cuts:
        result = result * levels(rng, dims, cuts, -0.22, 0.18)
    return jnp.clip(result, -limit, limit).astype(kind)


def setup_inputs(seed: int = 0) -> dict:
    key_of = jax.random.split(jax.random.key(seed), 5)
    return {
        "queries": draw_queries(jax.random.fold_in(key_of[4], 71), 0),
        "key_vectors": draw_key_vectors(jax.random.fold_in(key_of[4], 71), 0),
        "value_vectors": centred(key_of[2], (TOKENS, D), 1.0, 6.0, ((0, 32),)),
        "grad_output": centred(key_of[3], (TOKENS, D), 1.0, 6.0, ((0, 32),)),
    }


def tile_grads(query_rows, key_rows, value_rows, grad_rows, allowed):
    factor = HEAD_DIM ** -0.5
    best = lax.Precision.HIGHEST
    query_f = query_rows.astype(jnp.float32)
    key_f = key_rows.astype(jnp.float32)
    value_f = value_rows.astype(jnp.float32)
    grad_f = grad_rows.astype(jnp.float32)
    scores = jnp.einsum('rhe,che->hrc', query_f, key_f, precision=best) * factor
    scores = jnp.where(allowed[None], scores, -1e30)
    row_max = jnp.max(scores, axis=-1)
    log_total = row_max + jnp.log(jnp.sum(jnp.exp(scores - row_max[..., None]), axis=-1))
    attn_probs = jnp.exp(scores - log_total[..., None])
    probs_low = lax.optimization_barrier(attn_probs.astype(jnp.bfloat16)).astype(jnp.float32)
    attn_out = jnp.einsum('hrc,che->hre', probs_low, value_f, precision=best)
    row_dots = jnp.sum(jnp.transpose(grad_f, (1, 0, 2)) * attn_out, axis=-1)
    grad_probs = jnp.einsum('rhe,che->hrc', grad_f, value_f, precision=best)
    grad_scores = attn_probs * (grad_probs - row_dots[..., None])
    grad_scores = lax.optimization_barrier(grad_scores.astype(jnp.bfloat16)).astype(jnp.float32)
    grad_query = jnp.einsum('hrc,che->rhe', grad_scores, key_f, precision=best) * factor
    grad_key = jnp.einsum('hrc,rhe->che', grad_scores, query_f, precision=best) * factor
    grad_value = jnp.einsum('hrc,rhe->che', probs_low, grad_f, precision=best)
    return grad_query, grad_key, grad_value


def reference(queries, key_vectors, value_vectors, grad_output):
    token_count = queries.shape[0]
    blocks = token_count // WINDOW
    shape = (token_count, HEADS, HEAD_DIM)
    query_all = queries.reshape(shape)
    grad_all = grad_output.reshape(shape)
    front = jnp.zeros((WINDOW, HEADS, HEAD_DIM), jnp.bfloat16)
    key_all = jnp.concatenate([front, key_vectors.reshape(shape)], axis=0)
    value_all = jnp.concatenate([front, value_vectors.reshape(shape)], axis=0)
    row_ids = jnp.arange(WINDOW, dtype=jnp.int32)[:, None]
    col_ids = jnp.arange(2 * WINDOW, dtype=jnp.int32)[None, :]
    band = (col_ids > row_ids) & (col_ids <= row_ids + WINDOW)

    def one_block(block_index):
        start = (block_index * WINDOW).astype(jnp.int32)
        query_rows = lax.dynamic_slice_in_dim(query_all, start, WINDOW, 0)
        grad_rows = lax.dynamic_slice_in_dim(grad_all, start, WINDOW, 0)
        key_rows = lax.dynamic_slice_in_dim(key_all, start, 2 * WINDOW, 0)
        value_rows = lax.dynamic_slice_in_dim(value_all, start, 2 * WINDOW, 0)
        allowed = band & ((col_ids >= WINDOW) | (block_index > 0))
        grad_query, grad_key, grad_value = tile_grads(query_rows, key_rows, value_rows, grad_rows, allowed)
        return (grad_query.astype(jnp.bfloat16), grad_key[:WINDOW], grad_key[WINDOW:],
                grad_value[:WINDOW], grad_value[WINDOW:])

    grad_query, key_front, key_back, value_front, value_back = lax.map(one_block, jnp.arange(blocks, dtype=jnp.int32))
    grad_key = key_back + jnp.concatenate([key_front[1:], jnp.zeros_like(key_front[:1])], axis=0)
    grad_value = value_back + jnp.concatenate([value_front[1:], jnp.zeros_like(value_front[:1])], axis=0)
    width = HEADS * HEAD_DIM
    return (grad_query.reshape(token_count, width),
            grad_key.reshape(token_count, width).astype(jnp.bfloat16),
            grad_value.reshape(token_count, width).astype(jnp.bfloat16))
```

```python
import functools
import math

import jax
import jax.numpy as jnp
from jax import lax
from jax.experimental import pallas as pl
from jax.experimental.pallas import tpu as pltpu
from jax.sharding import Mesh, PartitionSpec as P

HEADS = 16
HEAD_DIM = 128
WINDOW = 512
TILE = 256
AXES = ("chunk", "part", "head")
GROUP = ("part", "head")
SCALE = HEAD_DIM ** (-0.5)
SCALE_LOG2 = SCALE * math.log2(math.e)
MASKED = -1e30
HBM = pl.BlockSpec(memory_space=pl.ANY)
VMEM_LIMIT = 48 * 1024 * 1024


def bf16(*shape):
    return jax.ShapeDtypeStruct(shape, jnp.bfloat16)


def f32(*shape):
    return jax.ShapeDtypeStruct(shape, jnp.float32)


def params():
    return pltpu.CompilerParams(vmem_limit_bytes=VMEM_LIMIT)


def group_index():
    return lax.axis_index("part") * lax.axis_size("head") + lax.axis_index("head")


def group_size():
    return lax.axis_size("part") * lax.axis_size("head")


def copy_all(pairs, sems):
    copies = [pltpu.make_async_copy(src, dst, sems.at[i]) for i, (src, dst) in enumerate(pairs)]
    for copy in copies:
        copy.start()
    for copy in copies:
        copy.wait()


def aligned(index, step):
    return pl.multiple_of(index * step, step)


def pack_kernel(n, *refs):
    q, k, v, g = refs[:4]
    crit = refs[4 : 4 + n]
    rest = refs[4 + n : 4 + 2 * n]
    sems = refs[-1]
    me = group_index()
    width = q.shape[1] // n
    late = me >= n // 2

    def send(first, second):
        pairs = []
        for out, pair in ((crit, first), (rest, second)):
            for m in range(n):
                cols = pl.ds(aligned(jnp.bitwise_xor(me, m), width), width)
                for t in range(2):
                    pairs.append((pair[t].at[:, cols], out[m].at[t]))
        copy_all(pairs, sems)

    @pl.when(late)
    def _():
        send((k, v), (q, g))

    @pl.when(jnp.logical_not(late))
    def _():
        send((q, g), (k, v))


def halo_kernel(n, *refs):
    crit = refs[:n]
    kv, qg = refs[n], refs[n + 1]
    sems = refs[-1]
    me = group_index()
    rows = crit[0].shape[1]
    ends = WINDOW // rows
    for phase in range(2):
        for m in range(n):
            other = jnp.bitwise_xor(me, m)

            @pl.when(other >= n - ends)
            def _():
                at = aligned(other - (n - ends), rows)
                copy = pltpu.make_async_copy(crit[m], kv.at[:, pl.ds(at, rows)], sems.at[m])
                copy.start() if phase == 0 else copy.wait()

            @pl.when(other < ends)
            def _():
                at = aligned(other, rows)
                copy = pltpu.make_async_copy(crit[m], qg.at[:, pl.ds(at, rows)], sems.at[m])
                copy.start() if phase == 0 else copy.wait()


def dot(a, b, dims):
    return lax.dot_general(a, b, (dims, ((), ())), preferred_element_type=jnp.float32)


NT = ((1,), (1,))
NN = ((1,), (0,))
TN = ((0,), (0,))


def main_kernel(n, heads, *refs):
    crit = refs[:n]
    rest = refs[n : 2 * n]
    kv_halo = refs[2 * n]
    dq_out = refs[2 * n + 1 : 3 * n + 1]
    front_out, back_out, stat_out = refs[3 * n + 1 : 3 * n + 4]
    x, dq, dk, dv, front, stat, sems = refs[3 * n + 4 :]
    me = group_index()
    first = lax.axis_index("chunk") == 0
    rows = crit[0].shape[1]
    total = n * rows
    pairs = [(kv_halo, x.at[pl.ds(2, 2), pl.ds(0, WINDOW)])]
    for m in range(n):
        other = jnp.bitwise_xor(me, m)
        kind = (other >= n // 2).astype(jnp.int32)
        at = pl.ds(pl.multiple_of(WINDOW + other * rows, rows), rows)
        pairs.append((crit[m], x.at[pl.ds(2 * kind, 2), at]))
        pairs.append((rest[m], x.at[pl.ds(2 - 2 * kind, 2), at]))
    copy_all(pairs, sems)
    stat[...] = jnp.zeros_like(stat)

    row = lax.broadcasted_iota(jnp.int32, (TILE, TILE), 0)
    col = lax.broadcasted_iota(jnp.int32, (TILE, TILE), 1)

    @pl.loop(0, total // TILE)
    def _(i):
        start = aligned(i, TILE)
        keys = pl.ds(start, 3 * TILE)
        mine = pl.ds(pl.multiple_of(WINDOW + start, TILE), TILE)
        low = jnp.where(first, WINDOW - start, 0)
        for h in range(heads):
            lanes = slice(h * HEAD_DIM, (h + 1) * HEAD_DIM)
            qb = x[0, mine, lanes]
            gb = x[1, mine, lanes]
            kb = x[2, keys, lanes]
            vb = x[3, keys, lanes]
            s = dot(kb, qb, NT) * SCALE_LOG2
            s0 = jnp.where(row > jnp.maximum(col, low - 1), s[:TILE], MASKED)
            s1 = jnp.where(row >= low - TILE, s[TILE : 2 * TILE], MASKED)
            s2 = jnp.where(row <= col, s[2 * TILE :], MASKED)
            s = jnp.concatenate([s0, s1, s2], axis=0)
            top = jnp.max(s, axis=0, keepdims=True)
            e = jnp.exp2(s - top)
            inverse = 1.0 / jnp.sum(e, axis=0, keepdims=True)
            p = e * inverse
            p_low = p.astype(jnp.bfloat16)
            dp = dot(vb, gb, NT)
            dots = jnp.sum(p_low.astype(jnp.float32) * dp, axis=0, keepdims=True)
            ds = (p * (dp - dots)).astype(jnp.bfloat16)
            dq[mine, lanes] = (dot(ds, kb, TN) * SCALE).astype(jnp.bfloat16)
            add_v = dot(p_low, gb, NN)
            add_k = dot(ds, qb, NN)
            older = pl.ds(start, 2 * TILE)
            dv[older, lanes] += add_v[: 2 * TILE]
            dk[older, lanes] += add_k[: 2 * TILE]
            dv[mine, lanes] = add_v[2 * TILE :]
            dk[mine, lanes] = add_k[2 * TILE :]

            @pl.when(i < WINDOW // TILE)
            def _():
                at = pl.ds(start, TILE)
                stat[3 * h : 3 * h + 1, at] = top
                stat[3 * h + 1 : 3 * h + 2, at] = inverse
                stat[3 * h + 2 : 3 * h + 3, at] = dots

    done = total - WINDOW
    front[0] = (dk[pl.ds(WINDOW, done)] * SCALE).astype(jnp.bfloat16)
    front[1] = dv[pl.ds(WINDOW, done)].astype(jnp.bfloat16)
    pairs = [
        (stat, stat_out),
        (front, front_out),
        (dk.at[pl.ds(total, WINDOW)], back_out.at[0]),
        (dv.at[pl.ds(total, WINDOW)], back_out.at[1]),
    ]
    for m in range(n):
        other = jnp.bitwise_xor(me, m)
        at = pl.ds(pl.multiple_of(WINDOW + other * rows, rows), rows)
        pairs.append((dq.at[at], dq_out[m]))
    copy_all(pairs, sems)


def edge_kernel(n, heads, *refs):
    crit = refs[:n]
    qg_halo, front_in, back_in, stat_in = refs[n : n + 4]
    out = refs[n + 4 : 2 * n + 4]
    kv, qg, full, back, stat, sems = refs[2 * n + 4 :]
    me = group_index()
    rows = crit[0].shape[1]
    total = n * rows
    done = total - WINDOW
    ends = WINDOW // rows
    for phase in range(2):
        for m in range(n):
            other = jnp.bitwise_xor(me, m)

            @pl.when(other >= n - ends)
            def _():
                at = aligned(other - (n - ends), rows)
                copy = pltpu.make_async_copy(crit[m], kv.at[:, pl.ds(at, rows)], sems.at[4 + m])
                copy.start() if phase == 0 else copy.wait()

        if phase == 0:
            copy_all(
                [(qg_halo, qg), (front_in, full.at[:, pl.ds(0, done)]), (back_in, back), (stat_in, stat)],
                sems,
            )

    row = lax.broadcasted_iota(jnp.int32, (TILE, TILE), 0)
    col = lax.broadcasted_iota(jnp.int32, (TILE, TILE), 1)
    for h in range(heads):
        lanes = slice(h * HEAD_DIM, (h + 1) * HEAD_DIM)
        for j in range(WINDOW // TILE):
            at = slice(j * TILE, (j + 1) * TILE)
            qb = qg[0, at, lanes]
            gb = qg[1, at, lanes]
            kb = kv[0, j * TILE :, lanes]
            vb = kv[1, j * TILE :, lanes]
            s = dot(kb, qb, NT) * SCALE_LOG2
            s0 = jnp.where(row > col, s[:TILE], MASKED)
            s = jnp.concatenate([s0, s[TILE:]], axis=0) if j == 0 else s0
            top = stat[3 * h : 3 * h + 1, at]
            inverse = stat[3 * h + 1 : 3 * h + 2, at]
            dots = stat[3 * h + 2 : 3 * h + 3, at]
            p = jnp.exp2(s - top) * inverse
            dp = dot(vb, gb, NT)
            ds = (p * (dp - dots)).astype(jnp.bfloat16)
            back[0, j * TILE :, lanes] += dot(ds, qb, NN)
            back[1, j * TILE :, lanes] += dot(p.astype(jnp.bfloat16), gb, NN)
    full[0, done:] = (back[0] * SCALE).astype(jnp.bfloat16)
    full[1, done:] = back[1].astype(jnp.bfloat16)
    pairs = []
    for m in range(n):
        at = pl.ds(aligned(jnp.bitwise_xor(me, m), rows), rows)
        pairs.append((full.at[:, at], out[m]))
    copy_all(pairs, sems)


def unpack_kernel(n, *refs):
    dq_in = refs[:n]
    dkv_in = refs[n : 2 * n]
    dq, dk, dv, sems = refs[2 * n :]
    me = group_index()
    width = dq_in[0].shape[1]
    pairs = []
    for m in range(n):
        cols = pl.ds(aligned(jnp.bitwise_xor(me, m), width), width)
        pairs.append((dq_in[m], dq.at[:, cols]))
        pairs.append((dkv_in[m].at[0], dk.at[:, cols]))
        pairs.append((dkv_in[m].at[1], dv.at[:, cols]))
    copy_all(pairs, sems)


def call(kernel, outs, scratch, sems, *operands):
    return pl.pallas_call(
        kernel,
        out_shape=outs,
        in_specs=[HBM] * len(operands),
        out_specs=jax.tree.map(lambda _: HBM, outs),
        scratch_shapes=[*scratch, pltpu.SemaphoreType.DMA((sems,))],
        compiler_params=params(),
    )(*operands)


def exchanged(pieces):
    n = len(pieces)
    return [pieces[0]] + [
        lax.ppermute(pieces[m], GROUP, [(i, i ^ m) for i in range(n)]) for m in range(1, n)
    ]


def per_device(queries, key_vectors, value_vectors, grad_output):
    n = group_size()
    chunks = lax.axis_size("chunk")
    rows, model = queries.shape
    heads = HEADS // n
    width = model // n
    total = n * rows
    piece = bf16(2, rows, width)
    packed = call(
        functools.partial(pack_kernel, n), [piece] * (2 * n), [], 4 * n,
        queries, key_vectors, value_vectors, grad_output,
    )
    crit = exchanged(packed[:n])
    end = bf16(2, WINDOW, width)
    kv_send, qg_send = call(functools.partial(halo_kernel, n), [end, end], [], n, *crit)
    forward = [(i, i + 1) for i in range(chunks - 1)]
    backward = [(i + 1, i) for i in range(chunks - 1)]
    kv_halo = lax.ppermute(kv_send, "chunk", forward)
    qg_halo = lax.ppermute(qg_send, "chunk", backward)
    rest = exchanged(packed[n:])
    done = total - WINDOW
    stat_rows = -(-3 * heads // 8) * 8
    *dq, front, back, stat = call(
        functools.partial(main_kernel, n, heads),
        [bf16(rows, width)] * n
        + [bf16(2, done, width), f32(2, WINDOW, width), f32(stat_rows, WINDOW)],
        [
            pltpu.VMEM((4, WINDOW + total, width), jnp.bfloat16),
            pltpu.VMEM((WINDOW + total, width), jnp.bfloat16),
            pltpu.VMEM((WINDOW + total, width), jnp.float32),
            pltpu.VMEM((WINDOW + total, width), jnp.float32),
            pltpu.VMEM((2, done, width), jnp.bfloat16),
            pltpu.VMEM((stat_rows, WINDOW), jnp.float32),
        ],
        2 * n + 4,
        *crit, *rest, kv_halo,
    )
    stat_halo = lax.ppermute(stat, "chunk", backward)
    dq = exchanged(dq)
    dkv = call(
        functools.partial(edge_kernel, n, heads),
        [piece] * n,
        [
            pltpu.VMEM((2, WINDOW, width), jnp.bfloat16),
            pltpu.VMEM((2, WINDOW, width), jnp.bfloat16),
            pltpu.VMEM((2, total, width), jnp.bfloat16),
            pltpu.VMEM((2, WINDOW, width), jnp.float32),
            pltpu.VMEM((stat_rows, WINDOW), jnp.float32),
        ],
        n + 4,
        *crit, qg_halo, front, back, stat_halo,
    )
    dkv = exchanged(dkv)
    out = bf16(rows, model)
    return tuple(
        call(functools.partial(unpack_kernel, n), [out] * 3, [], 3 * n, *dq, *dkv)
    )


def solution(mesh):
    seq, head = mesh.devices.shape
    part = max(1, min(seq, HEADS // 2 // head))
    fine = Mesh(mesh.devices.reshape(seq // part, part, head), AXES)
    placed = P(AXES, None)
    return jax.shard_map(
        per_device,
        mesh=fine,
        in_specs=(placed,) * 4,
        out_specs=(placed,) * 3,
        check_vma=False,
    )
```

```python
import functools
import math

import jax
import jax.numpy as jnp
from jax import lax
from jax.experimental import pallas as pl
from jax.experimental.pallas import tpu as pltpu
from jax.sharding import Mesh, PartitionSpec as P

HEADS = 16
HEAD_DIM = 128
WINDOW = 512
TILE = 256
HALF = 128
AXES = ("chunk", "part", "head")
GROUP = ("part", "head")
SCALE = HEAD_DIM ** (-0.5)
SCALE_LOG2 = SCALE * math.log2(math.e)
MASKED = -1e30
VMEM_LIMIT = 48 * 1024 * 1024
NT = ((1,), (1,))
NN = ((1,), (0,))
ORDER = (0, 1, 6, 7, 2, 4, 3, 5)
LATE_FLOPS = 16000000000
HALO_FLOPS = 0


def bf16(*shape):
    return jax.ShapeDtypeStruct(shape, jnp.bfloat16)


def f32(*shape):
    return jax.ShapeDtypeStruct(shape, jnp.float32)


def group_index():
    return lax.axis_index("part") * lax.axis_size("head") + lax.axis_index("head")


def group_size():
    return lax.axis_size("part") * lax.axis_size("head")


def aligned(index, step):
    return pl.multiple_of(index * step, step)


def copy_all(pairs, sems):
    copies = [pltpu.make_async_copy(src, dst, sems.at[i]) for i, (src, dst) in enumerate(pairs)]
    for copy in copies:
        copy.start()
    for copy in copies:
        copy.wait()


def copy_where(conditions, sems):
    for phase in range(2):
        for slot, flag, src, dst in conditions:

            @pl.when(flag)
            def _():
                copy = pltpu.make_async_copy(src, dst, sems.at[slot])
                copy.start() if phase == 0 else copy.wait()


def dot(a, b, dims):
    return lax.dot_general(a, b, (dims, ((), ())), preferred_element_type=jnp.float32)


def pack_kernel(n, *refs):
    sources = refs[:4]
    crit = refs[4 : 4 + n]
    rest = refs[4 + n : 4 + 2 * n]
    stage, sems = refs[4 + 2 * n :]
    me = group_index()
    width = stage.shape[2] // n
    late = (me >= n // 2).astype(jnp.int32)
    copy_all([(source, stage.at[i]) for i, source in enumerate(sources)], sems)
    pairs = []
    for m in range(n):
        cols = pl.ds(aligned(jnp.bitwise_xor(me, m), width), width)
        pairs.append((stage.at[pl.ds(2 * late, 2), :, cols], crit[m]))
        pairs.append((stage.at[pl.ds(2 - 2 * late, 2), :, cols], rest[m]))
    copy_all(pairs, sems)


def halo_kernel(n, *refs):
    crit = by_slot(refs[:n])
    kv, qg, sems = refs[n:]
    me = group_index()
    rows = crit[0].shape[1]
    ends = WINDOW // rows
    copies = []
    for m in range(n):
        other = jnp.bitwise_xor(me, m)
        at = pl.ds(aligned(other - (n - ends), rows), rows)
        copies.append((m, other >= n - ends, crit[m], kv.at[:, at]))
        at = pl.ds(aligned(other, rows), rows)
        copies.append((m, other < ends, crit[m], qg.at[:, at]))
    copy_where(copies, sems)


def softmax_block(qb, gb, kb, vb, bias, blind):
    row = lax.broadcasted_iota(jnp.int32, (HALF, HALF), 0)
    col = lax.broadcasted_iota(jnp.int32, (HALF, HALF), 1)
    s = dot(kb, qb, NT)
    dp = dot(vb, gb, NT)
    span = WINDOW // HALF + 1
    nothing = jnp.zeros((HALF, HALF), jnp.bfloat16)
    p_parts, ds_parts, stats = [], [], []
    for c in range(TILE // HALF):
        cols = slice(c * HALF, (c + 1) * HALF)
        parts = [s[(c + r) * HALF : (c + r + 1) * HALF, cols] for r in range(span)]
        parts[0] = jnp.where(row > col, parts[0], MASKED)
        parts[-1] = jnp.where(row <= col, parts[-1], MASKED)
        parts = [b + bias if (c + r) * HALF < blind else b for r, b in enumerate(parts)]
        sc = jnp.concatenate(parts, axis=0)
        dpc = dp[c * HALF : (c + span) * HALF, cols]
        top = jnp.max(sc, axis=0, keepdims=True) * SCALE_LOG2
        e = jnp.exp2(sc * SCALE_LOG2 - top)
        inverse = 1.0 / jnp.sum(e, axis=0, keepdims=True)
        p = e * inverse
        dots = jnp.sum(p * dpc, axis=0, keepdims=True)
        ds = (p * (dpc - dots)).astype(jnp.bfloat16)
        pad = [nothing] * c, [nothing] * (TILE // HALF - 1 - c)
        p_parts.append(jnp.concatenate([*pad[0], p.astype(jnp.bfloat16), *pad[1]], axis=0))
        ds_parts.append(jnp.concatenate([*pad[0], ds, *pad[1]], axis=0))
        stats.append((top, inverse, dots))
    return jnp.concatenate(p_parts, axis=1), jnp.concatenate(ds_parts, axis=1), stats


def late_kernel(n, heads, *refs):
    crit = by_slot(refs[:n])
    rest = by_slot(refs[n : 2 * n])
    dq_out, dkv_out, x, dq, dkv, sems = refs[2 * n :]
    me = group_index()
    rows = crit[0].shape[1]
    total = n * rows
    pairs = []
    for m in range(n):
        other = jnp.bitwise_xor(me, m)
        kind = (other >= n // 2).astype(jnp.int32)
        at = pl.ds(aligned(other, rows), rows)
        pairs.append((crit[m], x.at[pl.ds(2 * kind, 2), at]))
        pairs.append((rest[m], x.at[pl.ds(2 - 2 * kind, 2), at]))
    copy_all(pairs, sems)
    for h in range(heads):
        lanes = slice(h * HEAD_DIM, (h + 1) * HEAD_DIM)
        key_t = x[2, :, lanes].T
        for start in range(0, total - WINDOW, TILE):
            keys = slice(start, start + 3 * TILE)
            mine = slice(start + WINDOW, start + WINDOW + TILE)
            qb, gb = x[0, mine, lanes], x[1, mine, lanes]
            p_low, ds, _ = softmax_block(qb, gb, x[2, keys, lanes], x[3, keys, lanes], 0.0, 0)
            out = slice(start, start + TILE)
            dq[out, lanes] = (dot(key_t[:, keys], ds, NN) * SCALE).T.astype(jnp.bfloat16)
            for t, add in enumerate((dot(ds, qb, NN), dot(p_low, gb, NN))):
                if start == 0:
                    dkv[t, keys, lanes] = add
                else:
                    older = slice(start, start + 2 * TILE)
                    dkv[t, older, lanes] += add[: 2 * TILE]
                    dkv[t, mine, lanes] = add[2 * TILE :]
    copy_all([(dq, dq_out), (dkv, dkv_out)], sems)


def early_kernel(n, heads, *refs):
    crit = by_slot(refs[:n])
    rest = by_slot(refs[n : 2 * n])
    kv_halo, dq_in, dkv_in = refs[2 * n : 2 * n + 3]
    dq_out = refs[2 * n + 3 : 3 * n + 3]
    dkv_out, stat_out, x, dq, dkv, stat, sems = refs[3 * n + 3 :]
    me = group_index()
    first = lax.axis_index("chunk") == 0
    rows = crit[0].shape[1]
    total = n * rows
    ends = WINDOW // rows
    copies = []
    for m in range(n):
        other = jnp.bitwise_xor(me, m)
        need = other < ends
        at = pl.ds(aligned(other, rows), rows)
        copies.append((2 * m, need, crit[m], x.at[pl.ds(0, 2), at]))
        at = pl.ds(pl.multiple_of(WINDOW + other * rows, rows), rows)
        copies.append((2 * m + 1, need, rest[m], x.at[pl.ds(2, 2), at]))
    always = jnp.bool_(True)
    copies.append((2 * n, always, kv_halo, x.at[pl.ds(2, 2), pl.ds(0, WINDOW)]))
    copies.append((2 * n + 1, always, dkv_in.at[:, pl.ds(0, WINDOW)], dkv))
    copies.append((2 * n + 2, always, dq_in, dq.at[pl.ds(WINDOW, total - WINDOW)]))
    copy_where(copies, sems)
    stat[...] = jnp.zeros_like(stat)
    bias = jnp.where(first, MASKED, 0.0)
    for h in range(heads):
        lanes = slice(h * HEAD_DIM, (h + 1) * HEAD_DIM)
        key_t = x[2, :, lanes].T
        for start in range(0, WINDOW, TILE):
            keys = slice(start, start + 3 * TILE)
            mine = slice(start, start + TILE)
            qb, gb = x[0, mine, lanes], x[1, mine, lanes]
            p_low, ds, stats = softmax_block(
                qb, gb, x[2, keys, lanes], x[3, keys, lanes], bias, WINDOW - start
            )
            dq[mine, lanes] = (dot(key_t[:, keys], ds, NN) * SCALE).T.astype(jnp.bfloat16)
            own = slice(0, start + TILE)
            dkv[0, own, lanes] += dot(ds[WINDOW - start :], qb, NN)
            dkv[1, own, lanes] += dot(p_low[WINDOW - start :], gb, NN)
            for c, rows_of in enumerate(stats):
                at = slice(start + c * HALF, start + (c + 1) * HALF)
                for k, value in enumerate(rows_of):
                    stat[3 * h + k : 3 * h + k + 1, at] = value
    x[2, :WINDOW] = (dkv[0] * SCALE).astype(jnp.bfloat16)
    x[3, :WINDOW] = dkv[1].astype(jnp.bfloat16)
    pairs = [(stat, stat_out), (x.at[pl.ds(2, 2), pl.ds(0, WINDOW)], dkv_out)]
    for m in range(n):
        at = pl.ds(aligned(jnp.bitwise_xor(me, m), rows), rows)
        pairs.append((dq.at[at], dq_out[m]))
    copy_all(pairs, sems)


def edge_kernel(n, heads, *refs):
    crit = by_slot(refs[:n])
    qg_halo, front, dkv_in, stat_in = refs[n : n + 4]
    out = refs[n + 4 : 2 * n + 4]
    kv, qg, full, dkv, stat, sems = refs[2 * n + 4 :]
    me = group_index()
    rows = crit[0].shape[1]
    total = n * rows
    done = total - WINDOW
    ends = WINDOW // rows
    always = jnp.bool_(True)
    copies = [
        (n, always, qg_halo, qg),
        (n + 1, always, front, full.at[:, pl.ds(0, WINDOW)]),
        (n + 2, always, dkv_in.at[:, pl.ds(WINDOW, done)], dkv),
        (n + 3, always, stat_in, stat),
    ]
    for m in range(n):
        other = jnp.bitwise_xor(me, m)
        at = pl.ds(aligned(other - (n - ends), rows), rows)
        copies.append((m, other >= n - ends, crit[m], kv.at[:, at]))
    copy_where(copies, sems)
    row = lax.broadcasted_iota(jnp.int32, (TILE, TILE), 0)
    col = lax.broadcasted_iota(jnp.int32, (TILE, TILE), 1)
    for h in range(heads):
        lanes = slice(h * HEAD_DIM, (h + 1) * HEAD_DIM)
        for start in range(0, WINDOW, TILE):
            mine = slice(start, start + TILE)
            keys = slice(start, WINDOW)
            qb, gb = qg[0, mine, lanes], qg[1, mine, lanes]
            s = dot(kv[0, keys, lanes], qb, NT)
            newest = jnp.where(row > col, s[:TILE], MASKED)
            s = newest if len(s) == TILE else jnp.concatenate([newest, s[TILE:]], axis=0)
            top, inverse, dots = (stat[3 * h + k : 3 * h + k + 1, mine] for k in range(3))
            p = jnp.exp2(s * SCALE_LOG2 - top) * inverse
            dp = dot(kv[1, keys, lanes], gb, NT)
            ds = (p * (dp - dots)).astype(jnp.bfloat16)
            at = slice(done - WINDOW + start, done)
            dkv[0, at, lanes] += dot(ds, qb, NN)
            dkv[1, at, lanes] += dot(p.astype(jnp.bfloat16), gb, NN)
    full[0, WINDOW:] = (dkv[0] * SCALE).astype(jnp.bfloat16)
    full[1, WINDOW:] = dkv[1].astype(jnp.bfloat16)
    pairs = []
    for m in range(n):
        at = pl.ds(aligned(jnp.bitwise_xor(me, m), rows), rows)
        pairs.append((full.at[:, at], out[m]))
    copy_all(pairs, sems)


def unpack_kernel(n, *refs):
    dq_in = by_slot(refs[:n])
    dkv_in = by_slot(refs[n : 2 * n])
    dq, dk, dv, sems = refs[2 * n :]
    me = group_index()
    width = dq_in[0].shape[1]
    pairs = []
    for m in range(n):
        cols = pl.ds(aligned(jnp.bitwise_xor(me, m), width), width)
        pairs.append((dq_in[m], dq.at[:, cols]))
        pairs.append((dkv_in[m].at[0], dk.at[:, cols]))
        pairs.append((dkv_in[m].at[1], dv.at[:, cols]))
    copy_all(pairs, sems)


def call(kernel, outs, scratch, sems, *operands, space=pl.ANY, limit=VMEM_LIMIT, flops=0):
    return pl.pallas_call(
        kernel,
        out_shape=outs,
        in_specs=[pl.BlockSpec(memory_space=space)] * len(operands),
        out_specs=jax.tree.map(lambda _: pl.BlockSpec(memory_space=pl.ANY), outs),
        scratch_shapes=[*scratch, pltpu.SemaphoreType.DMA((sems,))],
        compiler_params=pltpu.CompilerParams(vmem_limit_bytes=limit),
        cost_estimate=pl.CostEstimate(flops=flops, bytes_accessed=0, transcendentals=0) if flops else None,
    )(*operands)


def vmem(shape):
    return pltpu.VMEM(shape.shape, shape.dtype)


def order_of(n):
    return [m for m in ORDER if m < n] + list(range(len(ORDER), n))


def by_slot(refs):
    order = order_of(len(refs))
    return [refs[order.index(m)] for m in range(len(refs))]


def exchanged(pieces):
    n = len(pieces)
    return [
        lax.ppermute(pieces[m], GROUP, [(i, i ^ m) for i in range(n)]) if m else pieces[0]
        for m in order_of(n)
    ]


def per_device(queries, key_vectors, value_vectors, grad_output):
    n = group_size()
    chunks = lax.axis_size("chunk")
    rows, model = queries.shape
    heads = HEADS // n
    width = model // n
    total = n * rows
    done = total - WINDOW
    piece = bf16(2, rows, width)
    packed = call(
        functools.partial(pack_kernel, n),
        [piece] * (2 * n),
        [vmem(bf16(4, rows, model))], 2 * n,
        queries, grad_output, key_vectors, value_vectors, space=pltpu.HBM, limit=None,
    )
    crit = exchanged(packed[:n])
    end = bf16(2, WINDOW, width)
    kv_send, qg_send = call(
        functools.partial(halo_kernel, n), [end, end], [], n, *crit, flops=HALO_FLOPS
    )
    forward = [(i, i + 1) for i in range(chunks - 1)]
    backward = [(i + 1, i) for i in range(chunks - 1)]
    kv_halo = lax.ppermute(kv_send, "chunk", forward)
    qg_halo = lax.ppermute(qg_send, "chunk", backward)
    rest = exchanged(packed[n:])
    stat_out = f32(-(-3 * heads // 8) * 8, WINDOW)
    partial_out = f32(2, total, width)
    dq_late, partial = call(
        functools.partial(late_kernel, n, heads),
        [bf16(done, width), partial_out],
        [vmem(bf16(4, total, width)), vmem(bf16(done, width)), vmem(partial_out)], 2 * n,
        *crit, *rest, flops=LATE_FLOPS,
    )
    *dq, front, stat = call(
        functools.partial(early_kernel, n, heads),
        [bf16(rows, width)] * n + [end, stat_out],
        [
            vmem(bf16(4, 2 * WINDOW, width)),
            vmem(bf16(total, width)),
            vmem(f32(2, WINDOW, width)),
            vmem(stat_out),
        ],
        2 * n + 3,
        *crit, *rest, kv_halo, dq_late, partial,
    )
    stat_halo = lax.ppermute(stat, "chunk", backward)
    dq = exchanged(dq)
    dkv = call(
        functools.partial(edge_kernel, n, heads),
        [piece] * n,
        [vmem(end), vmem(end), vmem(bf16(2, total, width)), vmem(f32(2, done, width)), vmem(stat_out)],
        n + 4,
        *crit, qg_halo, front, partial, stat_halo,
    )
    dkv = exchanged(dkv)
    out = bf16(rows, model)
    return tuple(
        call(functools.partial(unpack_kernel, n), [out] * 3, [], 3 * n, *dq, *dkv)
    )


def solution(mesh):
    seq, head = mesh.devices.shape
    part = max(1, min(seq, HEADS // 2 // head))
    fine = Mesh(mesh.devices.reshape(seq // part, part, head), AXES)
    placed = P(AXES, None)
    return jax.shard_map(
        per_device,
        mesh=fine,
        in_specs=(placed,) * 4,
        out_specs=(placed,) * 3,
        check_vma=False,
    )
```

```python
import functools
import math

import jax
import jax.numpy as jnp
from jax import lax
from jax.experimental import pallas as pl
from jax.experimental.pallas import tpu as pltpu
from jax.sharding import Mesh, PartitionSpec as P

HEADS = 16
HEAD_DIM = 128
WINDOW = 512
TILE = 256
HALF = 128
AXES = ("chunk", "part", "head")
GROUP = ("part", "head")
SCALE = HEAD_DIM ** (-0.5)
SCALE_LOG2 = SCALE * math.log2(math.e)
MASKED = -1e30
VMEM_LIMIT = 48 * 1024 * 1024
NT = ((1,), (1,))
NN = ((1,), (0,))
CRIT_ORDER = (0, 1, 6, 7, 2, 4, 3, 5)
REST_ORDER = (0, 1, 6, 7, 2, 4, 3, 5)
DQ_ORDER = (0, 1, 6, 7, 2, 4, 3, 5)
DKV_ORDER = (0, 1, 6, 7, 2, 4, 3, 5)
QG_FIRST = False
EDGE_FLOPS = 4000000000
LATE_FLOPS = 4000000000


def bf16(*shape):
    return jax.ShapeDtypeStruct(shape, jnp.bfloat16)


def f32(*shape):
    return jax.ShapeDtypeStruct(shape, jnp.float32)


def group_index():
    return lax.axis_index("part") * lax.axis_size("head") + lax.axis_index("head")


def group_size():
    return lax.axis_size("part") * lax.axis_size("head")


def aligned(index, step):
    return pl.multiple_of(index * step, step)


def copy_all(pairs, sems):
    copies = [pltpu.make_async_copy(src, dst, sems.at[i]) for i, (src, dst) in enumerate(pairs)]
    for copy in copies:
        copy.start()
    for copy in copies:
        copy.wait()


def dot(a, b, dims):
    return lax.dot_general(a, b, (dims, ((), ())), preferred_element_type=jnp.float32)


def pack_kernel(n, *refs):
    q, g, k, v = refs[:4]
    crit = refs[4 : 4 + n]
    rest = refs[4 + n : 4 + 2 * n]
    stage, sems = refs[4 + 2 * n :]
    me = group_index()
    width = stage.shape[2] // n

    def run(first, second):
        loads = [
            pltpu.make_async_copy(source, stage.at[i], sems.at[i])
            for i, source in enumerate((*first, *second))
        ]
        for load in loads:
            load.start()
        for i, load in enumerate(loads):
            load.wait()
            for m in range(n):
                cols = pl.ds(aligned(jnp.bitwise_xor(me, m), width), width)
                (crit if i < 2 else rest)[m][i % 2] = stage[i, :, cols]

    @pl.when(me >= n // 2)
    def _():
        run((k, v), (q, g))

    @pl.when(me < n // 2)
    def _():
        run((q, g), (k, v))


def place_all(pieces, late, early, me):
    n = len(pieces)
    rows = pieces[0].shape[1]

    def run(near, far):
        for m in range(n):
            at = pl.ds(aligned(jnp.bitwise_and(jnp.bitwise_xor(me, m), n // 2 - 1), rows), rows)
            (near if m < n // 2 else far)[:, at] = pieces[m][...]

    @pl.when(me >= n // 2)
    def _():
        run(late, early)

    @pl.when(me < n // 2)
    def _():
        run(early, late)


def halo_kernel(n, *refs):
    crit = by_slot(CRIT_ORDER, refs[:n])
    kv_late, qg_early, *sends = refs[n:]
    place_all(crit, kv_late, qg_early, group_index())
    if sends:
        sends[0][...] = kv_late[:, kv_late.shape[1] - WINDOW :]
        sends[1][...] = qg_early[:, :WINDOW]


def load(parts, t, lo, hi, lanes):
    out, start = [], 0
    for ref in parts:
        a, b = max(lo - start, 0), min(hi - start, ref.shape[1])
        if a < b:
            out.append(ref[t, a:b, lanes])
        start += ref.shape[1]
    return out[0] if len(out) == 1 else jnp.concatenate(out, axis=0)


def softmax_block(qb, gb, kb, vb, bias, blind):
    row = lax.broadcasted_iota(jnp.int32, (HALF, HALF), 0)
    col = lax.broadcasted_iota(jnp.int32, (HALF, HALF), 1)
    s = dot(kb, qb, NT)
    dp = dot(vb, gb, NT)
    span = WINDOW // HALF + 1
    nothing = jnp.zeros((HALF, HALF), jnp.bfloat16)
    p_parts, ds_parts, stats = [], [], []
    for c in range(TILE // HALF):
        cols = slice(c * HALF, (c + 1) * HALF)
        parts = [s[(c + r) * HALF : (c + r + 1) * HALF, cols] for r in range(span)]
        parts[0] = jnp.where(row > col, parts[0], MASKED)
        parts[-1] = jnp.where(row <= col, parts[-1], MASKED)
        parts = [b + bias if (c + r) * HALF < blind else b for r, b in enumerate(parts)]
        sc = jnp.concatenate(parts, axis=0)
        dpc = dp[c * HALF : (c + span) * HALF, cols]
        top = jnp.max(sc, axis=0, keepdims=True) * SCALE_LOG2
        e = jnp.exp2(sc * SCALE_LOG2 - top)
        inverse = 1.0 / jnp.sum(e, axis=0, keepdims=True)
        p = e * inverse
        dots = jnp.sum(p * dpc, axis=0, keepdims=True)
        ds = (p * (dpc - dots)).astype(jnp.bfloat16)
        pad = [nothing] * c, [nothing] * (TILE // HALF - 1 - c)
        p_parts.append(jnp.concatenate([*pad[0], p.astype(jnp.bfloat16), *pad[1]], axis=0))
        ds_parts.append(jnp.concatenate([*pad[0], ds, *pad[1]], axis=0))
        stats.append((top, inverse, dots))
    return jnp.concatenate(p_parts, axis=1), jnp.concatenate(ds_parts, axis=1), stats


def late_kernel(n, heads, *refs):
    rest = by_slot(REST_ORDER, refs[:n])
    kv_late, qg_early, qg_late, kv_early, dq, dkv = refs[n:]
    place_all(rest, qg_late, kv_early, group_index())
    total = dkv.shape[1]
    qg, kv = (qg_early, qg_late), (kv_early, kv_late)
    for h in range(heads):
        lanes = slice(h * HEAD_DIM, (h + 1) * HEAD_DIM)
        key_t = load(kv, 0, 0, total, lanes).T
        for start in range(0, total - WINDOW, TILE):
            keys = slice(start, start + 3 * TILE)
            mine = slice(start + WINDOW, start + WINDOW + TILE)
            qb, gb = (load(qg, t, start + WINDOW, start + WINDOW + TILE, lanes) for t in range(2))
            kb, vb = (load(kv, t, start, start + 3 * TILE, lanes) for t in range(2))
            p_low, ds, _ = softmax_block(qb, gb, kb, vb, 0.0, 0)
            out = slice(start, start + TILE)
            dq[out, lanes] = (dot(key_t[:, keys], ds, NN) * SCALE).T.astype(jnp.bfloat16)
            for t, add in enumerate((dot(ds, qb, NN), dot(p_low, gb, NN))):
                if start == 0:
                    dkv[t, keys, lanes] = add
                else:
                    older = slice(start, start + 2 * TILE)
                    dkv[t, older, lanes] += add[: 2 * TILE]
                    dkv[t, mine, lanes] = add[2 * TILE :]


def early_kernel(n, heads, *refs):
    qg_early, qg_late, kv_early, kv_late, kv_halo, dq_in, dkv_in = refs[:7]
    refs = refs[7 + QG_FIRST :]
    dq_out = refs[:n]
    front, stat, dq, acc = refs[n:]
    me = group_index()
    rows = dq_out[0].shape[0]
    first = lax.axis_index("chunk") == 0
    stat[...] = jnp.zeros_like(stat)
    dq[WINDOW:] = dq_in[...]
    acc[...] = dkv_in[:, :WINDOW]
    bias = jnp.where(first, MASKED, 0.0)
    qg, kv = (qg_early, qg_late), (kv_halo, kv_early, kv_late)
    for h in range(heads):
        lanes = slice(h * HEAD_DIM, (h + 1) * HEAD_DIM)
        key_t = load(kv, 0, 0, 2 * WINDOW, lanes).T
        for start in range(0, WINDOW, TILE):
            keys = slice(start, start + 3 * TILE)
            mine = slice(start, start + TILE)
            qb, gb = (load(qg, t, start, start + TILE, lanes) for t in range(2))
            kb, vb = (load(kv, t, start, start + 3 * TILE, lanes) for t in range(2))
            p_low, ds, stats = softmax_block(qb, gb, kb, vb, bias, WINDOW - start)
            dq[mine, lanes] = (dot(key_t[:, keys], ds, NN) * SCALE).T.astype(jnp.bfloat16)
            own = slice(0, start + TILE)
            acc[0, own, lanes] += dot(ds[WINDOW - start :], qb, NN)
            acc[1, own, lanes] += dot(p_low[WINDOW - start :], gb, NN)
            for c, rows_of in enumerate(stats):
                at = slice(start + c * HALF, start + (c + 1) * HALF)
                for k, value in enumerate(rows_of):
                    stat[3 * h + k : 3 * h + k + 1, at] = value
    for m in range(n):
        dq_out[m][...] = dq[pl.ds(aligned(jnp.bitwise_xor(me, m), rows), rows)]
    front[0] = (acc[0] * SCALE).astype(jnp.bfloat16)
    front[1] = acc[1].astype(jnp.bfloat16)


def edge_kernel(n, heads, *refs):
    kv_early, kv_late, qg, front, dkv_in, stat = refs[:6]
    out = refs[6 : 6 + n]
    full, acc = refs[6 + n :]
    me = group_index()
    total = dkv_in.shape[1]
    done = total - WINDOW
    rows = total // n
    kv = (kv_early, kv_late)
    row = lax.broadcasted_iota(jnp.int32, (TILE, TILE), 0)
    col = lax.broadcasted_iota(jnp.int32, (TILE, TILE), 1)
    acc[...] = dkv_in[:, WINDOW:]
    for h in range(heads):
        lanes = slice(h * HEAD_DIM, (h + 1) * HEAD_DIM)
        for start in range(0, WINDOW, TILE):
            mine = slice(start, start + TILE)
            qb, gb = qg[0, mine, lanes], qg[1, mine, lanes]
            kb, vb = (load(kv, t, done + start, total, lanes) for t in range(2))
            s = dot(kb, qb, NT)
            newest = jnp.where(row > col, s[:TILE], MASKED)
            s = newest if len(s) == TILE else jnp.concatenate([newest, s[TILE:]], axis=0)
            top, inverse, dots = (stat[3 * h + k : 3 * h + k + 1, mine] for k in range(3))
            p = jnp.exp2(s * SCALE_LOG2 - top) * inverse
            dp = dot(vb, gb, NT)
            ds = (p * (dp - dots)).astype(jnp.bfloat16)
            at = slice(done - WINDOW + start, done)
            acc[0, at, lanes] += dot(ds, qb, NN)
            acc[1, at, lanes] += dot(p.astype(jnp.bfloat16), gb, NN)
    full[:, :WINDOW] = front[...]
    full[0, WINDOW:] = (acc[0] * SCALE).astype(jnp.bfloat16)
    full[1, WINDOW:] = acc[1].astype(jnp.bfloat16)
    for m in range(n):
        out[m][...] = full[:, pl.ds(aligned(jnp.bitwise_xor(me, m), rows), rows)]


def unpack_kernel(n, *refs):
    dq_in = by_slot(DQ_ORDER, refs[:n])
    dkv_in = by_slot(DKV_ORDER, refs[n : 2 * n])
    dq, dk, dv, sems = refs[2 * n :]
    me = group_index()
    width = dq_in[0].shape[1]
    pairs = []
    for m in range(n):
        cols = pl.ds(aligned(jnp.bitwise_xor(me, m), width), width)
        pairs.append((dq_in[m], dq.at[:, cols]))
        pairs.append((dkv_in[m].at[0], dk.at[:, cols]))
        pairs.append((dkv_in[m].at[1], dv.at[:, cols]))
    copy_all(pairs, sems)


def call(kernel, outs, scratch, sems, *operands, space=pl.ANY, limit=VMEM_LIMIT, flops=0):
    held = pl.BlockSpec(memory_space=pltpu.VMEM)
    loose = pl.BlockSpec(memory_space=space)
    arrays = [x[0] if isinstance(x, tuple) else x for x in operands]
    return pl.pallas_call(
        kernel,
        out_shape=outs,
        in_specs=[held if isinstance(x, tuple) else loose for x in operands],
        out_specs=[held if not isinstance(x, jax.ShapeDtypeStruct) else pl.BlockSpec(memory_space=pl.ANY) for x in outs],
        scratch_shapes=[*scratch, *([pltpu.SemaphoreType.DMA((sems,))] if sems else [])],
        compiler_params=pltpu.CompilerParams(vmem_limit_bytes=limit),
        cost_estimate=pl.CostEstimate(flops=flops, bytes_accessed=0, transcendentals=0) if flops else None,
    )(*arrays)


def held(arrays):
    return [(x,) for x in arrays]


def vmem(shape):
    return pltpu.VMEM(shape.shape, shape.dtype)


def order_of(order, n):
    return [m for m in order if m < n] + list(range(len(order), n))


def by_slot(order, refs):
    order = order_of(order, len(refs))
    return [refs[order.index(m)] for m in range(len(refs))]


def exchanged(order, pieces):
    n = len(pieces)
    return [
        lax.ppermute(pieces[m], GROUP, [(i, i ^ m) for i in range(n)]) if m else pieces[0]
        for m in order_of(order, n)
    ]


def per_device(queries, key_vectors, value_vectors, grad_output):
    n = group_size()
    chunks = lax.axis_size("chunk")
    rows, model = queries.shape
    heads = HEADS // n
    width = model // n
    total = n * rows
    done = total - WINDOW
    piece = bf16(2, rows, width)
    packed = call(
        functools.partial(pack_kernel, n),
        [vmem(piece)] * (2 * n),
        [vmem(bf16(4, rows, model))], 4,
        queries, grad_output, key_vectors, value_vectors, space=pltpu.HBM, limit=None,
    )
    crit = exchanged(CRIT_ORDER, packed[:n])
    half = total // 2
    end = vmem(bf16(2, WINDOW, width))
    halves = vmem(bf16(2, half, width))
    sends = call(
        functools.partial(halo_kernel, n),
        [halves, halves] + [end, end] * (half > WINDOW), [], 0, *held(crit),
    )
    kv_late, qg_early = sends[:2]
    kv_send, qg_send = sends[-2:]
    forward = [(i, i + 1) for i in range(chunks - 1)]
    backward = [(i + 1, i) for i in range(chunks - 1)]
    kv_halo = lax.ppermute(kv_send, "chunk", forward)
    qg_halo = lax.ppermute(qg_send, "chunk", backward)
    rest = exchanged(REST_ORDER, packed[n:])
    stat_out = vmem(f32(-(-3 * heads // 8) * 8, WINDOW))
    qg_late, kv_early, dq_late, partial = call(
        functools.partial(late_kernel, n, heads),
        [halves, halves, vmem(bf16(done, width)), vmem(f32(2, total, width))],
        [], 0,
        *held(rest), (kv_late,), (qg_early,), flops=LATE_FLOPS,
    )
    *dq, front, stat = call(
        functools.partial(early_kernel, n, heads),
        [vmem(bf16(rows, width))] * n + [end, stat_out],
        [vmem(bf16(total, width)), vmem(f32(2, WINDOW, width))], 0,
        *held((qg_early, qg_late, kv_early, kv_late, kv_halo, dq_late, partial)),
        *([qg_halo] if QG_FIRST else []),
    )
    stat_halo = lax.ppermute(stat, "chunk", backward)
    dq = exchanged(DQ_ORDER, dq)
    dkv = call(
        functools.partial(edge_kernel, n, heads),
        [vmem(piece)] * n, [vmem(bf16(2, total, width)), vmem(f32(2, done, width))], 0,
        *held((kv_early, kv_late, qg_halo, front, partial, stat_halo)), flops=EDGE_FLOPS,
    )
    dkv = exchanged(DKV_ORDER, dkv)
    out = bf16(rows, model)
    return tuple(
        call(functools.partial(unpack_kernel, n), [out] * 3, [], 3 * n, *held(dq), *held(dkv))
    )


def solution(mesh):
    seq, head = mesh.devices.shape
    part = max(1, min(seq, HEADS // 2 // head))
    fine = Mesh(mesh.devices.reshape(seq // part, part, head), AXES)
    placed = P(AXES, None)
    return jax.shard_map(
        per_device,
        mesh=fine,
        in_specs=(placed,) * 4,
        out_specs=(placed,) * 3,
        check_vma=False,
    )
```

```python
import functools
import math

import jax
import jax.numpy as jnp
from jax import lax
from jax.experimental import pallas as pl
from jax.experimental.pallas import tpu as pltpu
from jax.sharding import Mesh, PartitionSpec as P

HEADS = 16
HEAD_DIM = 128
WINDOW = 512
TILE = 256
HALF = 128
AXES = ("chunk", "part", "head")
GROUP = ("part", "head")
SCALE = HEAD_DIM ** (-0.5)
SCALE_LOG2 = SCALE * math.log2(math.e)
MASKED = -1e30
VMEM_LIMIT = 48 * 1024 * 1024
NT = ((1,), (1,))
NN = ((1,), (0,))
CRIT_ORDER = (0, 6, 7, 2, 4, 1, 3, 5)
REST_ORDER = (0, 3, 5, 1, 6, 7, 2, 4)
DQ_ORDER = (0, 3, 1, 2)
DKV_ORDER = (0, 6, 2, 4, 7, 3, 5, 1)
QG_FIRST = False
EDGE_FLOPS = 4000000000
LATE_FLOPS = 4000000000


def bf16(*shape):
    return jax.ShapeDtypeStruct(shape, jnp.bfloat16)


def f32(*shape):
    return jax.ShapeDtypeStruct(shape, jnp.float32)


def group_index():
    return lax.axis_index("part") * lax.axis_size("head") + lax.axis_index("head")


def group_size():
    return lax.axis_size("part") * lax.axis_size("head")


def aligned(index, step):
    return pl.multiple_of(index * step, step)


def copy_all(pairs, sems):
    copies = [pltpu.make_async_copy(src, dst, sems.at[i]) for i, (src, dst) in enumerate(pairs)]
    for copy in copies:
        copy.start()
    for copy in copies:
        copy.wait()


def dot(a, b, dims):
    return lax.dot_general(a, b, (dims, ((), ())), preferred_element_type=jnp.float32)


def pack_kernel(n, *refs):
    q, g, k, v = refs[:4]
    crit = refs[4 : 4 + n]
    rest = refs[4 + n : 4 + 2 * n]
    stage, sems = refs[4 + 2 * n :]
    me = group_index()
    width = stage.shape[2] // n

    def run(first, second):
        loads = [
            pltpu.make_async_copy(source, stage.at[i], sems.at[i])
            for i, source in enumerate((*first, *second))
        ]
        for load in loads:
            load.start()
        for i, load in enumerate(loads):
            load.wait()
            for m in range(n):
                cols = pl.ds(aligned(jnp.bitwise_xor(me, m), width), width)
                (crit if i < 2 else rest)[m][i % 2] = stage[i, :, cols]

    @pl.when(me >= n // 2)
    def _():
        run((k, v), (q, g))

    @pl.when(me < n // 2)
    def _():
        run((q, g), (k, v))


def place_all(pieces, late, early, me):
    n = len(pieces)
    rows = pieces[0].shape[1]

    def run(near, far):
        for m in range(n):
            at = pl.ds(aligned(jnp.bitwise_and(jnp.bitwise_xor(me, m), n // 2 - 1), rows), rows)
            (near if m < n // 2 else far)[:, at] = pieces[m][...]

    @pl.when(me >= n // 2)
    def _():
        run(late, early)

    @pl.when(me < n // 2)
    def _():
        run(early, late)


def halo_kernel(n, *refs):
    crit = by_slot(CRIT_ORDER, refs[:n])
    kv_late, qg_early, *sends = refs[n:]
    place_all(crit, kv_late, qg_early, group_index())
    if sends:
        sends[0][...] = kv_late[:, kv_late.shape[1] - WINDOW :]
        sends[1][...] = qg_early[:, :WINDOW]


def load(parts, t, lo, hi, lanes):
    out, start = [], 0
    for ref in parts:
        a, b = max(lo - start, 0), min(hi - start, ref.shape[1])
        if a < b:
            out.append(ref[t, a:b, lanes])
        start += ref.shape[1]
    return out[0] if len(out) == 1 else jnp.concatenate(out, axis=0)


def softmax_block(qb, gb, kb, vb, bias, blind):
    row = lax.broadcasted_iota(jnp.int32, (HALF, HALF), 0)
    col = lax.broadcasted_iota(jnp.int32, (HALF, HALF), 1)
    s = dot(kb, qb, NT)
    dp = dot(vb, gb, NT)
    span = WINDOW // HALF + 1
    nothing = jnp.zeros((HALF, HALF), jnp.bfloat16)
    p_parts, ds_parts, stats = [], [], []
    for c in range(TILE // HALF):
        cols = slice(c * HALF, (c + 1) * HALF)
        parts = [s[(c + r) * HALF : (c + r + 1) * HALF, cols] for r in range(span)]
        parts[0] = jnp.where(row > col, parts[0], MASKED)
        parts[-1] = jnp.where(row <= col, parts[-1], MASKED)
        parts = [b + bias if (c + r) * HALF < blind else b for r, b in enumerate(parts)]
        sc = jnp.concatenate(parts, axis=0)
        dpc = dp[c * HALF : (c + span) * HALF, cols]
        top = jnp.max(sc, axis=0, keepdims=True) * SCALE_LOG2
        e = jnp.exp2(sc * SCALE_LOG2 - top)
        inverse = 1.0 / jnp.sum(e, axis=0, keepdims=True)
        p = e * inverse
        dots = jnp.sum(p * dpc, axis=0, keepdims=True)
        ds = (p * (dpc - dots)).astype(jnp.bfloat16)
        pad = [nothing] * c, [nothing] * (TILE // HALF - 1 - c)
        p_parts.append(jnp.concatenate([*pad[0], p.astype(jnp.bfloat16), *pad[1]], axis=0))
        ds_parts.append(jnp.concatenate([*pad[0], ds, *pad[1]], axis=0))
        stats.append((top, inverse, dots))
    return jnp.concatenate(p_parts, axis=1), jnp.concatenate(ds_parts, axis=1), stats


def late_kernel(n, heads, *refs):
    rest = by_slot(REST_ORDER, refs[:n])
    kv_late, qg_early, qg_late, kv_early, dq, dkv = refs[n:]
    place_all(rest, qg_late, kv_early, group_index())
    total = dkv.shape[1]
    qg, kv = (qg_early, qg_late), (kv_early, kv_late)
    for h in range(heads):
        lanes = slice(h * HEAD_DIM, (h + 1) * HEAD_DIM)
        key_t = load(kv, 0, 0, total, lanes).T
        for start in range(0, total - WINDOW, TILE):
            keys = slice(start, start + 3 * TILE)
            mine = slice(start + WINDOW, start + WINDOW + TILE)
            qb, gb = (load(qg, t, start + WINDOW, start + WINDOW + TILE, lanes) for t in range(2))
            kb, vb = (load(kv, t, start, start + 3 * TILE, lanes) for t in range(2))
            p_low, ds, _ = softmax_block(qb, gb, kb, vb, 0.0, 0)
            out = slice(start, start + TILE)
            dq[out, lanes] = (dot(key_t[:, keys], ds, NN) * SCALE).T.astype(jnp.bfloat16)
            for t, add in enumerate((dot(ds, qb, NN), dot(p_low, gb, NN))):
                if start == 0:
                    dkv[t, keys, lanes] = add
                else:
                    older = slice(start, start + 2 * TILE)
                    dkv[t, older, lanes] += add[: 2 * TILE]
                    dkv[t, mine, lanes] = add[2 * TILE :]


def early_kernel(n, heads, *refs):
    qg_early, qg_late, kv_early, kv_late, kv_halo, dq_in, dkv_in = refs[:7]
    refs = refs[7 + QG_FIRST :]
    dq_out = refs[: n // 2]
    front, stat, dq, acc = refs[n // 2 :]
    me = group_index()
    rows = dq_out[0].shape[1]
    first = lax.axis_index("chunk") == 0
    stat[...] = jnp.zeros_like(stat)
    dq[WINDOW:] = dq_in[...]
    acc[...] = dkv_in[:, :WINDOW]
    bias = jnp.where(first, MASKED, 0.0)
    qg, kv = (qg_early, qg_late), (kv_halo, kv_early, kv_late)
    for h in range(heads):
        lanes = slice(h * HEAD_DIM, (h + 1) * HEAD_DIM)
        key_t = load(kv, 0, 0, 2 * WINDOW, lanes).T
        for start in range(0, WINDOW, TILE):
            keys = slice(start, start + 3 * TILE)
            mine = slice(start, start + TILE)
            qb, gb = (load(qg, t, start, start + TILE, lanes) for t in range(2))
            kb, vb = (load(kv, t, start, start + 3 * TILE, lanes) for t in range(2))
            p_low, ds, stats = softmax_block(qb, gb, kb, vb, bias, WINDOW - start)
            dq[mine, lanes] = (dot(key_t[:, keys], ds, NN) * SCALE).T.astype(jnp.bfloat16)
            own = slice(0, start + TILE)
            acc[0, own, lanes] += dot(ds[WINDOW - start :], qb, NN)
            acc[1, own, lanes] += dot(p_low[WINDOW - start :], gb, NN)
            for c, rows_of in enumerate(stats):
                at = slice(start + c * HALF, start + (c + 1) * HALF)
                for k, value in enumerate(rows_of):
                    stat[3 * h + k : 3 * h + k + 1, at] = value
    for m in range(n):
        dq_out[m // 2][m % 2] = dq[pl.ds(aligned(jnp.bitwise_xor(me, m), rows), rows)]
    front[0] = (acc[0] * SCALE).astype(jnp.bfloat16)
    front[1] = acc[1].astype(jnp.bfloat16)


def edge_kernel(n, heads, *refs):
    kv_early, kv_late, qg, front, dkv_in, stat = refs[:6]
    out = refs[6 : 6 + n]
    full, acc = refs[6 + n :]
    me = group_index()
    total = dkv_in.shape[1]
    done = total - WINDOW
    rows = total // n
    kv = (kv_early, kv_late)
    row = lax.broadcasted_iota(jnp.int32, (TILE, TILE), 0)
    col = lax.broadcasted_iota(jnp.int32, (TILE, TILE), 1)
    acc[...] = dkv_in[:, WINDOW:]
    for h in range(heads):
        lanes = slice(h * HEAD_DIM, (h + 1) * HEAD_DIM)
        for start in range(0, WINDOW, TILE):
            mine = slice(start, start + TILE)
            qb, gb = qg[0, mine, lanes], qg[1, mine, lanes]
            kb, vb = (load(kv, t, done + start, total, lanes) for t in range(2))
            s = dot(kb, qb, NT)
            newest = jnp.where(row > col, s[:TILE], MASKED)
            s = newest if len(s) == TILE else jnp.concatenate([newest, s[TILE:]], axis=0)
            top, inverse, dots = (stat[3 * h + k : 3 * h + k + 1, mine] for k in range(3))
            p = jnp.exp2(s * SCALE_LOG2 - top) * inverse
            dp = dot(vb, gb, NT)
            ds = (p * (dp - dots)).astype(jnp.bfloat16)
            at = slice(done - WINDOW + start, done)
            acc[0, at, lanes] += dot(ds, qb, NN)
            acc[1, at, lanes] += dot(p.astype(jnp.bfloat16), gb, NN)
    full[:, :WINDOW] = front[...]
    full[0, WINDOW:] = (acc[0] * SCALE).astype(jnp.bfloat16)
    full[1, WINDOW:] = acc[1].astype(jnp.bfloat16)
    for m in range(n):
        out[m][...] = full[:, pl.ds(aligned(jnp.bitwise_xor(me, m), rows), rows)]


def core_kernel(*refs):
    *pieces, out = refs
    for slot, piece in enumerate(by_slot(DQ_ORDER, pieces)):
        out[slot] = piece[1]


def unpack_kernel(n, *refs):
    chips = n // 2
    dq_in = by_slot(DQ_ORDER, refs[:chips])
    other = refs[chips]
    dkv_in = by_slot(DKV_ORDER, refs[chips + 1 : chips + 1 + n])
    dq, dk, dv, sems = refs[chips + 1 + n :]
    me = group_index()
    width = other.shape[2]
    pairs = []
    for m in range(n):
        cols = pl.ds(aligned(jnp.bitwise_xor(me, m), width), width)
        pairs.append((other.at[m // 2] if m % 2 else dq_in[m // 2].at[0], dq.at[:, cols]))
        pairs.append((dkv_in[m].at[0], dk.at[:, cols]))
        pairs.append((dkv_in[m].at[1], dv.at[:, cols]))
    copy_all(pairs, sems)


def call(kernel, outs, scratch, sems, *operands, space=pl.ANY, limit=VMEM_LIMIT, flops=0):
    held = pl.BlockSpec(memory_space=pltpu.VMEM)
    loose = pl.BlockSpec(memory_space=space)
    arrays = [x[0] if isinstance(x, tuple) else x for x in operands]
    return pl.pallas_call(
        kernel,
        out_shape=outs,
        in_specs=[held if isinstance(x, tuple) else loose for x in operands],
        out_specs=[held if not isinstance(x, jax.ShapeDtypeStruct) else pl.BlockSpec(memory_space=pl.ANY) for x in outs],
        scratch_shapes=[*scratch, *([pltpu.SemaphoreType.DMA((sems,))] if sems else [])],
        compiler_params=pltpu.CompilerParams(vmem_limit_bytes=limit),
        cost_estimate=pl.CostEstimate(flops=flops, bytes_accessed=0, transcendentals=0) if flops else None,
    )(*arrays)


def held(arrays):
    return [(x,) for x in arrays]


def vmem(shape):
    return pltpu.VMEM(shape.shape, shape.dtype)


def order_of(order, n):
    return [m for m in order if m < n] + list(range(len(order), n))


def by_slot(order, refs):
    order = order_of(order, len(refs))
    return [refs[order.index(m)] for m in range(len(refs))]


def exchanged(order, pieces, step=1):
    n = len(pieces)
    return [
        lax.ppermute(pieces[m], GROUP, [(i, i ^ (step * m)) for i in range(step * n)]) if m else pieces[0]
        for m in order_of(order, n)
    ]


def per_device(queries, key_vectors, value_vectors, grad_output):
    n = group_size()
    chunks = lax.axis_size("chunk")
    rows, model = queries.shape
    heads = HEADS // n
    width = model // n
    total = n * rows
    done = total - WINDOW
    piece = bf16(2, rows, width)
    packed = call(
        functools.partial(pack_kernel, n),
        [vmem(piece)] * (2 * n),
        [vmem(bf16(4, rows, model))], 4,
        queries, grad_output, key_vectors, value_vectors, space=pltpu.HBM, limit=None,
    )
    crit = exchanged(CRIT_ORDER, packed[:n])
    half = total // 2
    end = vmem(bf16(2, WINDOW, width))
    halves = vmem(bf16(2, half, width))
    sends = call(
        functools.partial(halo_kernel, n),
        [halves, halves] + [end, end] * (half > WINDOW), [], 0, *held(crit),
    )
    kv_late, qg_early = sends[:2]
    kv_send, qg_send = sends[-2:]
    forward = [(i, i + 1) for i in range(chunks - 1)]
    backward = [(i + 1, i) for i in range(chunks - 1)]
    kv_halo = lax.ppermute(kv_send, "chunk", forward)
    qg_halo = lax.ppermute(qg_send, "chunk", backward)
    rest = exchanged(REST_ORDER, packed[n:])
    stat_out = vmem(f32(-(-3 * heads // 8) * 8, WINDOW))
    qg_late, kv_early, dq_late, partial = call(
        functools.partial(late_kernel, n, heads),
        [halves, halves, vmem(bf16(done, width)), vmem(f32(2, total, width))],
        [], 0,
        *held(rest), (kv_late,), (qg_early,), flops=LATE_FLOPS,
    )
    *dq, front, stat = call(
        functools.partial(early_kernel, n, heads),
        [vmem(bf16(2, rows, width))] * (n // 2) + [end, stat_out],
        [vmem(bf16(total, width)), vmem(f32(2, WINDOW, width))], 0,
        *held((qg_early, qg_late, kv_early, kv_late, kv_halo, dq_late, partial)),
        *([qg_halo] if QG_FIRST else []),
    )
    stat_halo = lax.ppermute(stat, "chunk", backward)
    dq = exchanged(DQ_ORDER, dq, 2)
    other, = call(
        core_kernel, [vmem(bf16(n // 2, rows, width))], [], 0, *held(dq)
    )
    other = lax.ppermute(other, GROUP, [(i, i ^ 1) for i in range(n)])
    dkv = call(
        functools.partial(edge_kernel, n, heads),
        [vmem(piece)] * n, [vmem(bf16(2, total, width)), vmem(f32(2, done, width))], 0,
        *held((kv_early, kv_late, qg_halo, front, partial, stat_halo)), flops=EDGE_FLOPS,
    )
    dkv = exchanged(DKV_ORDER, dkv)
    out = bf16(rows, model)
    return tuple(
        call(functools.partial(unpack_kernel, n), [out] * 3, [], 3 * n, *held(dq), (other,), *held(dkv))
    )


def solution(mesh):
    seq, head = mesh.devices.shape
    part = max(1, min(seq, HEADS // 2 // head))
    fine = Mesh(mesh.devices.reshape(seq // part, part, head), AXES)
    placed = P(AXES, None)
    return jax.shard_map(
        per_device,
        mesh=fine,
        in_specs=(placed,) * 4,
        out_specs=(placed,) * 3,
        check_vma=False,
    )
```

```python
import functools
import math

import jax
import jax.numpy as jnp
from jax import lax
from jax.experimental import pallas as pl
from jax.experimental.pallas import tpu as pltpu
from jax.sharding import Mesh, PartitionSpec as P

HEADS = 16
HEAD_DIM = 128
WINDOW = 512
TILE = 256
HALF = 128
AXES = ("chunk", "part", "head")
GROUP = ("part", "head")
SCALE = HEAD_DIM ** (-0.5)
SCALE_LOG2 = SCALE * math.log2(math.e)
MASKED = -1e30
VMEM_LIMIT = 48 * 1024 * 1024
NT = ((1,), (1,))
NN = ((1,), (0,))
CRIT_ORDER = (0, 6, 7, 2, 4, 1, 3, 5)
REST_ORDER = (0, 3, 5, 1, 6, 7, 2, 4)
DQ_ORDER = (0, 3, 1, 2)
DKV_ORDER = (0, 6, 2, 4, 7, 3, 5, 1)
DEPTH = 2
EDGE_FLOPS = 4000000000
LATE_FLOPS = 4000000000


def bf16(*shape):
    return jax.ShapeDtypeStruct(shape, jnp.bfloat16)


def f32(*shape):
    return jax.ShapeDtypeStruct(shape, jnp.float32)


def group_index():
    return lax.axis_index("part") * lax.axis_size("head") + lax.axis_index("head")


def group_size():
    return lax.axis_size("part") * lax.axis_size("head")


def aligned(index, step):
    return pl.multiple_of(index * step, step)


def copy_all(pairs, sems):
    copies = [pltpu.make_async_copy(src, dst, sems.at[i]) for i, (src, dst) in enumerate(pairs)]
    for copy in copies:
        copy.start()
    for copy in copies:
        copy.wait()


def dot(a, b, dims):
    return lax.dot_general(a, b, (dims, ((), ())), preferred_element_type=jnp.float32)


def pack_kernel(n, *refs):
    q, g, k, v = refs[:4]
    crit = refs[4 : 4 + n]
    rest = refs[4 + n : 4 + 2 * n]
    stage, sems = refs[4 + 2 * n :]
    me = group_index()
    width = stage.shape[2] // n

    def run(first, second):
        loads = [
            pltpu.make_async_copy(source, stage.at[i], sems.at[i])
            for i, source in enumerate((*first, *second))
        ]
        for load in loads:
            load.start()
        for i, load in enumerate(loads):
            load.wait()
            for m in range(n):
                cols = pl.ds(aligned(jnp.bitwise_xor(me, m), width), width)
                (crit if i < 2 else rest)[m][i % 2] = stage[i, :, cols]

    @pl.when(me >= n // 2)
    def _():
        run((k, v), (q, g))

    @pl.when(me < n // 2)
    def _():
        run((q, g), (k, v))


def place_all(pieces, late, early, me):
    n = len(pieces)
    rows = pieces[0].shape[1]

    def run(near, far):
        for m in range(n):
            at = pl.ds(aligned(jnp.bitwise_and(jnp.bitwise_xor(me, m), n // 2 - 1), rows), rows)
            (near if m < n // 2 else far)[:, at] = pieces[m][...]

    @pl.when(me >= n // 2)
    def _():
        run(late, early)

    @pl.when(me < n // 2)
    def _():
        run(early, late)


def halo_kernel(n, *refs):
    crit = by_slot(CRIT_ORDER, refs[:n])
    kv_late, qg_early, *sends = refs[n:]
    place_all(crit, kv_late, qg_early, group_index())
    if sends:
        sends[0][...] = kv_late[:, kv_late.shape[1] - WINDOW :]
        sends[1][...] = qg_early[:, :WINDOW]


def load(parts, t, lo, hi, lanes):
    out, start = [], 0
    for ref in parts:
        a, b = max(lo - start, 0), min(hi - start, ref.shape[1])
        if a < b:
            out.append(ref[t, a:b, lanes])
        start += ref.shape[1]
    return out[0] if len(out) == 1 else jnp.concatenate(out, axis=0)


def softmax_block(s, dp, bias, blind):
    row = lax.broadcasted_iota(jnp.int32, (HALF, HALF), 0)
    col = lax.broadcasted_iota(jnp.int32, (HALF, HALF), 1)
    span = WINDOW // HALF + 1
    nothing = jnp.zeros((HALF, HALF), jnp.bfloat16)
    p_parts, ds_parts, stats = [], [], []
    for c in range(TILE // HALF):
        cols = slice(c * HALF, (c + 1) * HALF)
        parts = [s[(c + r) * HALF : (c + r + 1) * HALF, cols] for r in range(span)]
        parts[0] = jnp.where(row > col, parts[0], MASKED)
        parts[-1] = jnp.where(row <= col, parts[-1], MASKED)
        parts = [b + bias if (c + r) * HALF < blind else b for r, b in enumerate(parts)]
        sc = jnp.concatenate(parts, axis=0)
        dpc = dp[c * HALF : (c + span) * HALF, cols]
        top = jnp.max(sc, axis=0, keepdims=True) * SCALE_LOG2
        e = jnp.exp2(sc * SCALE_LOG2 - top)
        inverse = 1.0 / jnp.sum(e, axis=0, keepdims=True)
        p = e * inverse
        dots = jnp.sum(p * dpc, axis=0, keepdims=True)
        ds = (p * (dpc - dots)).astype(jnp.bfloat16)
        pad = [nothing] * c, [nothing] * (TILE // HALF - 1 - c)
        p_parts.append(jnp.concatenate([*pad[0], p.astype(jnp.bfloat16), *pad[1]], axis=0))
        ds_parts.append(jnp.concatenate([*pad[0], ds, *pad[1]], axis=0))
        stats.append((top, inverse, dots))
    return jnp.concatenate(p_parts, axis=1), jnp.concatenate(ds_parts, axis=1), stats


def staged(blocks, first, second, third):
    made, held_back = {}, {}
    for i in range(len(blocks) + DEPTH):
        if i < len(blocks):
            made[i] = first(*blocks[i])
        j = i - DEPTH // 2
        if 0 <= j < len(blocks):
            held_back[j] = second(*blocks[j], *made.pop(j))
        k = i - DEPTH
        if 0 <= k < len(blocks):
            third(*blocks[k], *held_back.pop(k))


def late_kernel(n, heads, *refs):
    rest = by_slot(REST_ORDER, refs[:n])
    kv_late, qg_early, qg_late, kv_early, dq, dkv = refs[n:]
    place_all(rest, qg_late, kv_early, group_index())
    total = dkv.shape[1]
    qg, kv = (qg_early, qg_late), (kv_early, kv_late)
    blocks = [(h, start) for h in range(heads) for start in range(0, total - WINDOW, TILE)]
    lanes_of = [slice(h * HEAD_DIM, (h + 1) * HEAD_DIM) for h in range(heads)]
    key_ts = [load(kv, 0, 0, total, lanes).T for lanes in lanes_of]

    def products(h, start):
        qb, gb = (load(qg, t, start + WINDOW, start + WINDOW + TILE, lanes_of[h]) for t in range(2))
        kb, vb = (load(kv, t, start, start + 3 * TILE, lanes_of[h]) for t in range(2))
        return dot(kb, qb, NT), dot(vb, gb, NT)

    def gradients(h, start, p_low, ds):
        lanes = lanes_of[h]
        keys = slice(start, start + 3 * TILE)
        mine = slice(start + WINDOW, start + WINDOW + TILE)
        qb, gb = (load(qg, t, start + WINDOW, start + WINDOW + TILE, lanes) for t in range(2))
        dq[slice(start, start + TILE), lanes] = (
            (dot(key_ts[h][:, keys], ds, NN) * SCALE).T.astype(jnp.bfloat16)
        )
        for t, add in enumerate((dot(ds, qb, NN), dot(p_low, gb, NN))):
            if start == 0:
                dkv[t, keys, lanes] = add
            else:
                older = slice(start, start + 2 * TILE)
                dkv[t, older, lanes] += add[: 2 * TILE]
                dkv[t, mine, lanes] = add[2 * TILE :]

    staged(blocks, products, lambda h, start, s, dp: softmax_block(s, dp, 0.0, 0)[:2], gradients)


def early_kernel(n, heads, *refs):
    qg_early, qg_late, kv_early, kv_late, kv_halo, dq_in, dkv_in = refs[:7]
    refs = refs[7:]
    dq_out = refs[: n // 2]
    front, stat, dq, acc = refs[n // 2 :]
    me = group_index()
    rows = dq_out[0].shape[1]
    first = lax.axis_index("chunk") == 0
    stat[...] = jnp.zeros_like(stat)
    dq[WINDOW:] = dq_in[...]
    acc[...] = dkv_in[:, :WINDOW]
    bias = jnp.where(first, MASKED, 0.0)
    qg, kv = (qg_early, qg_late), (kv_halo, kv_early, kv_late)
    blocks = [(h, start) for h in range(heads) for start in range(0, WINDOW, TILE)]
    lanes_of = [slice(h * HEAD_DIM, (h + 1) * HEAD_DIM) for h in range(heads)]
    key_ts = [load(kv, 0, 0, 2 * WINDOW, lanes).T for lanes in lanes_of]

    def products(h, start):
        qb, gb = (load(qg, t, start, start + TILE, lanes_of[h]) for t in range(2))
        kb, vb = (load(kv, t, start, start + 3 * TILE, lanes_of[h]) for t in range(2))
        return dot(kb, qb, NT), dot(vb, gb, NT)

    def probabilities(h, start, s, dp):
        p_low, ds, stats = softmax_block(s, dp, bias, WINDOW - start)
        for c, rows_of in enumerate(stats):
            at = slice(start + c * HALF, start + (c + 1) * HALF)
            for k, value in enumerate(rows_of):
                stat[3 * h + k : 3 * h + k + 1, at] = value
        return p_low, ds

    def gradients(h, start, p_low, ds):
        lanes = lanes_of[h]
        keys = slice(start, start + 3 * TILE)
        qb, gb = (load(qg, t, start, start + TILE, lanes) for t in range(2))
        dq[slice(start, start + TILE), lanes] = (
            (dot(key_ts[h][:, keys], ds, NN) * SCALE).T.astype(jnp.bfloat16)
        )
        own = slice(0, start + TILE)
        acc[0, own, lanes] += dot(ds[WINDOW - start :], qb, NN)
        acc[1, own, lanes] += dot(p_low[WINDOW - start :], gb, NN)

    staged(blocks, products, probabilities, gradients)
    for m in range(n):
        dq_out[m // 2][m % 2] = dq[pl.ds(aligned(jnp.bitwise_xor(me, m), rows), rows)]
    front[0] = (acc[0] * SCALE).astype(jnp.bfloat16)
    front[1] = acc[1].astype(jnp.bfloat16)


def edge_kernel(n, heads, *refs):
    kv_early, kv_late, qg, front, dkv_in, stat = refs[:6]
    out = refs[6 : 6 + n]
    full, acc = refs[6 + n :]
    me = group_index()
    total = dkv_in.shape[1]
    done = total - WINDOW
    rows = total // n
    kv = (kv_early, kv_late)
    row = lax.broadcasted_iota(jnp.int32, (TILE, TILE), 0)
    col = lax.broadcasted_iota(jnp.int32, (TILE, TILE), 1)
    acc[...] = dkv_in[:, WINDOW:]
    for h in range(heads):
        lanes = slice(h * HEAD_DIM, (h + 1) * HEAD_DIM)
        for start in range(0, WINDOW, TILE):
            mine = slice(start, start + TILE)
            qb, gb = qg[0, mine, lanes], qg[1, mine, lanes]
            kb, vb = (load(kv, t, done + start, total, lanes) for t in range(2))
            s = dot(kb, qb, NT)
            newest = jnp.where(row > col, s[:TILE], MASKED)
            s = newest if len(s) == TILE else jnp.concatenate([newest, s[TILE:]], axis=0)
            top, inverse, dots = (stat[3 * h + k : 3 * h + k + 1, mine] for k in range(3))
            p = jnp.exp2(s * SCALE_LOG2 - top) * inverse
            dp = dot(vb, gb, NT)
            ds = (p * (dp - dots)).astype(jnp.bfloat16)
            at = slice(done - WINDOW + start, done)
            acc[0, at, lanes] += dot(ds, qb, NN)
            acc[1, at, lanes] += dot(p.astype(jnp.bfloat16), gb, NN)
    full[:, :WINDOW] = front[...]
    full[0, WINDOW:] = (acc[0] * SCALE).astype(jnp.bfloat16)
    full[1, WINDOW:] = acc[1].astype(jnp.bfloat16)
    for m in range(n):
        out[m][...] = full[:, pl.ds(aligned(jnp.bitwise_xor(me, m), rows), rows)]


def core_kernel(*refs):
    *pieces, out = refs
    for slot, piece in enumerate(by_slot(DQ_ORDER, pieces)):
        out[slot] = piece[1]


def unpack_kernel(n, *refs):
    chips = n // 2
    dq_in = by_slot(DQ_ORDER, refs[:chips])
    other = refs[chips]
    dkv_in = by_slot(DKV_ORDER, refs[chips + 1 : chips + 1 + n])
    dq, dk, dv, sems = refs[chips + 1 + n :]
    me = group_index()
    width = other.shape[2]
    pairs = []
    for m in range(n):
        cols = pl.ds(aligned(jnp.bitwise_xor(me, m), width), width)
        pairs.append((other.at[m // 2] if m % 2 else dq_in[m // 2].at[0], dq.at[:, cols]))
        pairs.append((dkv_in[m].at[0], dk.at[:, cols]))
        pairs.append((dkv_in[m].at[1], dv.at[:, cols]))
    copy_all(pairs, sems)


def call(kernel, outs, scratch, sems, *operands, space=pl.ANY, limit=VMEM_LIMIT, flops=0):
    held = pl.BlockSpec(memory_space=pltpu.VMEM)
    loose = pl.BlockSpec(memory_space=space)
    arrays = [x[0] if isinstance(x, tuple) else x for x in operands]
    return pl.pallas_call(
        kernel,
        out_shape=outs,
        in_specs=[held if isinstance(x, tuple) else loose for x in operands],
        out_specs=[held if not isinstance(x, jax.ShapeDtypeStruct) else pl.BlockSpec(memory_space=pl.ANY) for x in outs],
        scratch_shapes=[*scratch, *([pltpu.SemaphoreType.DMA((sems,))] if sems else [])],
        compiler_params=pltpu.CompilerParams(vmem_limit_bytes=limit),
        cost_estimate=pl.CostEstimate(flops=flops, bytes_accessed=0, transcendentals=0) if flops else None,
    )(*arrays)


def held(arrays):
    return [(x,) for x in arrays]


def vmem(shape):
    return pltpu.VMEM(shape.shape, shape.dtype)


def order_of(order, n):
    return [m for m in order if m < n] + list(range(len(order), n))


def by_slot(order, refs):
    order = order_of(order, len(refs))
    return [refs[order.index(m)] for m in range(len(refs))]


def exchanged(order, pieces, step=1):
    n = len(pieces)
    return [
        lax.ppermute(pieces[m], GROUP, [(i, i ^ (step * m)) for i in range(step * n)]) if m else pieces[0]
        for m in order_of(order, n)
    ]


def per_device(queries, key_vectors, value_vectors, grad_output):
    n = group_size()
    chunks = lax.axis_size("chunk")
    rows, model = queries.shape
    heads = HEADS // n
    width = model // n
    total = n * rows
    done = total - WINDOW
    piece = bf16(2, rows, width)
    packed = call(
        functools.partial(pack_kernel, n),
        [vmem(piece)] * (2 * n),
        [vmem(bf16(4, rows, model))], 4,
        queries, grad_output, key_vectors, value_vectors, space=pltpu.HBM, limit=None,
    )
    crit = exchanged(CRIT_ORDER, packed[:n])
    half = total // 2
    end = vmem(bf16(2, WINDOW, width))
    halves = vmem(bf16(2, half, width))
    sends = call(
        functools.partial(halo_kernel, n),
        [halves, halves] + [end, end] * (half > WINDOW), [], 0, *held(crit),
    )
    kv_late, qg_early = sends[:2]
    kv_send, qg_send = sends[-2:]
    forward = [(i, i + 1) for i in range(chunks - 1)]
    backward = [(i + 1, i) for i in range(chunks - 1)]
    kv_halo = lax.ppermute(kv_send, "chunk", forward)
    qg_halo = lax.ppermute(qg_send, "chunk", backward)
    rest = exchanged(REST_ORDER, packed[n:])
    stat_out = vmem(f32(-(-3 * heads // 8) * 8, WINDOW))
    qg_late, kv_early, dq_late, partial = call(
        functools.partial(late_kernel, n, heads),
        [halves, halves, vmem(bf16(done, width)), vmem(f32(2, total, width))],
        [], 0,
        *held(rest), (kv_late,), (qg_early,), flops=LATE_FLOPS,
    )
    *dq, front, stat = call(
        functools.partial(early_kernel, n, heads),
        [vmem(bf16(2, rows, width))] * (n // 2) + [end, stat_out],
        [vmem(bf16(total, width)), vmem(f32(2, WINDOW, width))], 0,
        *held((qg_early, qg_late, kv_early, kv_late, kv_halo, dq_late, partial)),
    )
    stat_halo = lax.ppermute(stat, "chunk", backward)
    dq = exchanged(DQ_ORDER, dq, 2)
    other, = call(
        core_kernel, [vmem(bf16(n // 2, rows, width))], [], 0, *held(dq)
    )
    other = lax.ppermute(other, GROUP, [(i, i ^ 1) for i in range(n)])
    dkv = call(
        functools.partial(edge_kernel, n, heads),
        [vmem(piece)] * n, [vmem(bf16(2, total, width)), vmem(f32(2, done, width))], 0,
        *held((kv_early, kv_late, qg_halo, front, partial, stat_halo)), flops=EDGE_FLOPS,
    )
    dkv = exchanged(DKV_ORDER, dkv)
    out = bf16(rows, model)
    return tuple(
        call(functools.partial(unpack_kernel, n), [out] * 3, [], 3 * n, *held(dq), (other,), *held(dkv))
    )


def solution(mesh):
    seq, head = mesh.devices.shape
    part = max(1, min(seq, HEADS // 2 // head))
    fine = Mesh(mesh.devices.reshape(seq // part, part, head), AXES)
    placed = P(AXES, None)
    return jax.shard_map(
        per_device,
        mesh=fine,
        in_specs=(placed,) * 4,
        out_specs=(placed,) * 3,
        check_vma=False,
    )
```

```python
import functools
import math

import jax
import jax.numpy as jnp
from jax import lax
from jax.experimental import pallas as pl
from jax.experimental.pallas import tpu as pltpu
from jax.sharding import Mesh, PartitionSpec as P

HEADS = 16
HEAD_DIM = 128
WINDOW = 512
TILE = 256
HALF = 128
AXES = ("chunk", "part", "head")
GROUP = ("part", "head")
SCALE = HEAD_DIM ** (-0.5)
SCALE_LOG2 = SCALE * math.log2(math.e)
MASKED = -1e30
VMEM_LIMIT = 48 * 1024 * 1024
NT = ((1,), (1,))
NN = ((1,), (0,))
CRIT_ORDER = (0, 6, 7, 2, 4, 1, 3, 5)
REST_ORDER = (0, 3, 5, 1, 6, 7, 2, 4)
DQ_ORDER = (0, 2, 1, 3)
DKV_ORDER = (0, 7, 3, 4, 6, 2, 5, 1)
DEPTH = 2
EDGE_FLOPS = 4000000000
LATE_FLOPS = 4000000000


def bf16(*shape):
    return jax.ShapeDtypeStruct(shape, jnp.bfloat16)


def f32(*shape):
    return jax.ShapeDtypeStruct(shape, jnp.float32)


def group_index():
    return lax.axis_index("part") * lax.axis_size("head") + lax.axis_index("head")


def group_size():
    return lax.axis_size("part") * lax.axis_size("head")


def aligned(index, step):
    return pl.multiple_of(index * step, step)


def copy_all(pairs, sems):
    copies = [pltpu.make_async_copy(src, dst, sems.at[i]) for i, (src, dst) in enumerate(pairs)]
    for copy in copies:
        copy.start()
    for copy in copies:
        copy.wait()


def dot(a, b, dims):
    return lax.dot_general(a, b, (dims, ((), ())), preferred_element_type=jnp.float32)


def pack_kernel(n, late_pair, early_pair, *refs):
    out = refs[4 : 4 + n]
    stage, sems = refs[4 + n :]
    me = group_index()
    width = stage.shape[2] // n

    def run(pair):
        loads = [
            pltpu.make_async_copy(refs[source], stage.at[t], sems.at[t])
            for t, source in enumerate(pair)
        ]
        for load in loads:
            load.start()
        for t, load in enumerate(loads):
            load.wait()
            for m in range(n):
                cols = pl.ds(aligned(jnp.bitwise_xor(me, m), width), width)
                out[m][t] = stage[t, :, cols]

    @pl.when(me >= n // 2)
    def _():
        run(late_pair)

    @pl.when(me < n // 2)
    def _():
        run(early_pair)


def place_all(pieces, late, early, me):
    n = len(pieces)
    rows = pieces[0].shape[1]

    def run(near, far):
        for m in range(n):
            at = pl.ds(aligned(jnp.bitwise_and(jnp.bitwise_xor(me, m), n // 2 - 1), rows), rows)
            (near if m < n // 2 else far)[:, at] = pieces[m][...]

    @pl.when(me >= n // 2)
    def _():
        run(late, early)

    @pl.when(me < n // 2)
    def _():
        run(early, late)


def halo_kernel(n, *refs):
    crit = by_slot(CRIT_ORDER, refs[:n])
    kv_late, qg_early, *sends = refs[n:]
    place_all(crit, kv_late, qg_early, group_index())
    if sends:
        sends[0][...] = kv_late[:, kv_late.shape[1] - WINDOW :]
        sends[1][...] = qg_early[:, :WINDOW]


def load(parts, t, lo, hi, lanes):
    out, start = [], 0
    for ref in parts:
        a, b = max(lo - start, 0), min(hi - start, ref.shape[1])
        if a < b:
            out.append(ref[t, a:b, lanes])
        start += ref.shape[1]
    return out[0] if len(out) == 1 else jnp.concatenate(out, axis=0)


def softmax_block(s, dp, bias, blind):
    row = lax.broadcasted_iota(jnp.int32, (HALF, HALF), 0)
    col = lax.broadcasted_iota(jnp.int32, (HALF, HALF), 1)
    span = WINDOW // HALF + 1
    nothing = jnp.zeros((HALF, HALF), jnp.bfloat16)
    p_parts, ds_parts, stats = [], [], []
    for c in range(TILE // HALF):
        cols = slice(c * HALF, (c + 1) * HALF)
        parts = [s[(c + r) * HALF : (c + r + 1) * HALF, cols] for r in range(span)]
        parts[0] = jnp.where(row > col, parts[0], MASKED)
        parts[-1] = jnp.where(row <= col, parts[-1], MASKED)
        parts = [b + bias if (c + r) * HALF < blind else b for r, b in enumerate(parts)]
        sc = jnp.concatenate(parts, axis=0)
        dpc = dp[c * HALF : (c + span) * HALF, cols]
        top = jnp.max(sc, axis=0, keepdims=True) * SCALE_LOG2
        e = jnp.exp2(sc * SCALE_LOG2 - top)
        inverse = 1.0 / jnp.sum(e, axis=0, keepdims=True)
        p = e * inverse
        dots = jnp.sum(p * dpc, axis=0, keepdims=True)
        ds = (p * (dpc - dots)).astype(jnp.bfloat16)
        pad = [nothing] * c, [nothing] * (TILE // HALF - 1 - c)
        p_parts.append(jnp.concatenate([*pad[0], p.astype(jnp.bfloat16), *pad[1]], axis=0))
        ds_parts.append(jnp.concatenate([*pad[0], ds, *pad[1]], axis=0))
        stats.append((top, inverse, dots))
    return jnp.concatenate(p_parts, axis=1), jnp.concatenate(ds_parts, axis=1), stats


def staged(blocks, first, second, third):
    made, held_back = {}, {}
    for i in range(len(blocks) + DEPTH):
        if i < len(blocks):
            made[i] = first(*blocks[i])
        j = i - DEPTH // 2
        if 0 <= j < len(blocks):
            held_back[j] = second(*blocks[j], *made.pop(j))
        k = i - DEPTH
        if 0 <= k < len(blocks):
            third(*blocks[k], *held_back.pop(k))


def late_kernel(n, heads, *refs):
    rest = by_slot(REST_ORDER, refs[:n])
    kv_late, qg_early, qg_late, kv_early, dq, dkv = refs[n:]
    place_all(rest, qg_late, kv_early, group_index())
    total = dkv.shape[1]
    qg, kv = (qg_early, qg_late), (kv_early, kv_late)
    blocks = [(h, start) for h in range(heads) for start in range(0, total - WINDOW, TILE)]
    lanes_of = [slice(h * HEAD_DIM, (h + 1) * HEAD_DIM) for h in range(heads)]
    key_ts = [load(kv, 0, 0, total, lanes).T for lanes in lanes_of]

    def products(h, start):
        qb, gb = (load(qg, t, start + WINDOW, start + WINDOW + TILE, lanes_of[h]) for t in range(2))
        kb, vb = (load(kv, t, start, start + 3 * TILE, lanes_of[h]) for t in range(2))
        return dot(kb, qb, NT), dot(vb, gb, NT)

    def gradients(h, start, p_low, ds):
        lanes = lanes_of[h]
        keys = slice(start, start + 3 * TILE)
        mine = slice(start + WINDOW, start + WINDOW + TILE)
        qb, gb = (load(qg, t, start + WINDOW, start + WINDOW + TILE, lanes) for t in range(2))
        dq[slice(start, start + TILE), lanes] = (
            (dot(key_ts[h][:, keys], ds, NN) * SCALE).T.astype(jnp.bfloat16)
        )
        for t, add in enumerate((dot(ds, qb, NN), dot(p_low, gb, NN))):
            if start == 0:
                dkv[t, keys, lanes] = add
            else:
                older = slice(start, start + 2 * TILE)
                dkv[t, older, lanes] += add[: 2 * TILE]
                dkv[t, mine, lanes] = add[2 * TILE :]

    staged(blocks, products, lambda h, start, s, dp: softmax_block(s, dp, 0.0, 0)[:2], gradients)


def early_kernel(n, heads, *refs):
    qg_early, qg_late, kv_early, kv_late, kv_halo, dq_in, dkv_in = refs[:7]
    refs = refs[7:]
    dq_out = refs[: n // 2]
    front, stat, dq, acc = refs[n // 2 :]
    me = group_index()
    rows = dq_out[0].shape[1]
    first = lax.axis_index("chunk") == 0
    stat[...] = jnp.zeros_like(stat)
    dq[WINDOW:] = dq_in[...]
    acc[...] = dkv_in[:, :WINDOW]
    bias = jnp.where(first, MASKED, 0.0)
    qg, kv = (qg_early, qg_late), (kv_halo, kv_early, kv_late)
    blocks = [(h, start) for h in range(heads) for start in range(0, WINDOW, TILE)]
    lanes_of = [slice(h * HEAD_DIM, (h + 1) * HEAD_DIM) for h in range(heads)]
    key_ts = [load(kv, 0, 0, 2 * WINDOW, lanes).T for lanes in lanes_of]

    def products(h, start):
        qb, gb = (load(qg, t, start, start + TILE, lanes_of[h]) for t in range(2))
        kb, vb = (load(kv, t, start, start + 3 * TILE, lanes_of[h]) for t in range(2))
        return dot(kb, qb, NT), dot(vb, gb, NT)

    def probabilities(h, start, s, dp):
        p_low, ds, stats = softmax_block(s, dp, bias, WINDOW - start)
        for c, rows_of in enumerate(stats):
            at = slice(start + c * HALF, start + (c + 1) * HALF)
            for k, value in enumerate(rows_of):
                stat[3 * h + k : 3 * h + k + 1, at] = value
        return p_low, ds

    def gradients(h, start, p_low, ds):
        lanes = lanes_of[h]
        keys = slice(start, start + 3 * TILE)
        qb, gb = (load(qg, t, start, start + TILE, lanes) for t in range(2))
        dq[slice(start, start + TILE), lanes] = (
            (dot(key_ts[h][:, keys], ds, NN) * SCALE).T.astype(jnp.bfloat16)
        )
        own = slice(0, start + TILE)
        acc[0, own, lanes] += dot(ds[WINDOW - start :], qb, NN)
        acc[1, own, lanes] += dot(p_low[WINDOW - start :], gb, NN)

    staged(blocks, products, probabilities, gradients)
    for m in range(n):
        dq_out[m // 2][m % 2] = dq[pl.ds(aligned(jnp.bitwise_xor(me, m), rows), rows)]
    front[0] = (acc[0] * SCALE).astype(jnp.bfloat16)
    front[1] = acc[1].astype(jnp.bfloat16)


def edge_kernel(n, heads, *refs):
    kv_early, kv_late, qg, front, dkv_in, stat = refs[:6]
    refs = refs[6:]
    out = refs[:n]
    full, acc = refs[n:]
    me = group_index()
    total = dkv_in.shape[1]
    done = total - WINDOW
    rows = total // n
    kv = (kv_early, kv_late)
    row = lax.broadcasted_iota(jnp.int32, (TILE, TILE), 0)
    col = lax.broadcasted_iota(jnp.int32, (TILE, TILE), 1)
    acc[...] = dkv_in[:, WINDOW:]
    for h in range(heads):
        lanes = slice(h * HEAD_DIM, (h + 1) * HEAD_DIM)
        for start in range(0, WINDOW, TILE):
            mine = slice(start, start + TILE)
            qb, gb = qg[0, mine, lanes], qg[1, mine, lanes]
            kb, vb = (load(kv, t, done + start, total, lanes) for t in range(2))
            s = dot(kb, qb, NT)
            newest = jnp.where(row > col, s[:TILE], MASKED)
            s = newest if len(s) == TILE else jnp.concatenate([newest, s[TILE:]], axis=0)
            top, inverse, dots = (stat[3 * h + k : 3 * h + k + 1, mine] for k in range(3))
            p = jnp.exp2(s * SCALE_LOG2 - top) * inverse
            dp = dot(vb, gb, NT)
            ds = (p * (dp - dots)).astype(jnp.bfloat16)
            at = slice(done - WINDOW + start, done)
            acc[0, at, lanes] += dot(ds, qb, NN)
            acc[1, at, lanes] += dot(p.astype(jnp.bfloat16), gb, NN)
    full[:, :WINDOW] = front[...]
    full[0, WINDOW:] = (acc[0] * SCALE).astype(jnp.bfloat16)
    full[1, WINDOW:] = acc[1].astype(jnp.bfloat16)
    for m in range(n):
        out[m][...] = full[:, pl.ds(aligned(jnp.bitwise_xor(me, m), rows), rows)]


def core_kernel(*refs):
    *pieces, out = refs
    for slot, piece in enumerate(by_slot(DQ_ORDER, pieces)):
        out[slot] = piece[1]


def unpack_kernel(n, *refs):
    chips = n // 2
    dq_in = by_slot(DQ_ORDER, refs[:chips])
    other = refs[chips]
    dkv_in = by_slot(DKV_ORDER, refs[chips + 1 : chips + 1 + n])
    dq, dk, dv, sems = refs[chips + 1 + n :]
    me = group_index()
    width = other.shape[2]
    pairs = []
    for m in range(n):
        cols = pl.ds(aligned(jnp.bitwise_xor(me, m), width), width)
        pairs.append((other.at[m // 2] if m % 2 else dq_in[m // 2].at[0], dq.at[:, cols]))
        pairs.append((dkv_in[m].at[0], dk.at[:, cols]))
        pairs.append((dkv_in[m].at[1], dv.at[:, cols]))
    copy_all(pairs, sems)


def call(kernel, outs, scratch, sems, *operands, space=pl.ANY, limit=VMEM_LIMIT, flops=0):
    held = pl.BlockSpec(memory_space=pltpu.VMEM)
    loose = pl.BlockSpec(memory_space=space)
    arrays = [x[0] if isinstance(x, tuple) else x for x in operands]
    return pl.pallas_call(
        kernel,
        out_shape=outs,
        in_specs=[held if isinstance(x, tuple) else loose for x in operands],
        out_specs=[held if not isinstance(x, jax.ShapeDtypeStruct) else pl.BlockSpec(memory_space=pl.ANY) for x in outs],
        scratch_shapes=[*scratch, *([pltpu.SemaphoreType.DMA((sems,))] if sems else [])],
        compiler_params=pltpu.CompilerParams(vmem_limit_bytes=limit),
        cost_estimate=pl.CostEstimate(flops=flops, bytes_accessed=0, transcendentals=0) if flops else None,
    )(*arrays)


def held(arrays):
    return [(x,) for x in arrays]


def vmem(shape):
    return pltpu.VMEM(shape.shape, shape.dtype)


def order_of(order, n):
    return [m for m in order if m < n] + list(range(len(order), n))


def by_slot(order, refs):
    order = order_of(order, len(refs))
    return [refs[order.index(m)] for m in range(len(refs))]


def exchanged(order, pieces, step=1):
    n = len(pieces)
    return [
        lax.ppermute(pieces[m], GROUP, [(i, i ^ (step * m)) for i in range(step * n)]) if m else pieces[0]
        for m in order_of(order, n)
    ]


def per_device(queries, key_vectors, value_vectors, grad_output):
    n = group_size()
    chunks = lax.axis_size("chunk")
    rows, model = queries.shape
    heads = HEADS // n
    width = model // n
    total = n * rows
    done = total - WINDOW
    piece = bf16(2, rows, width)
    arguments = (queries, grad_output, key_vectors, value_vectors)

    def packed(late_pair, early_pair):
        return call(
            functools.partial(pack_kernel, n, late_pair, early_pair), [vmem(piece)] * n,
            [vmem(bf16(2, rows, model))], 2, *arguments, space=pltpu.HBM, limit=None,
        )

    crit = exchanged(CRIT_ORDER, packed((2, 3), (0, 1)))
    half = total // 2
    end = vmem(bf16(2, WINDOW, width))
    halves = vmem(bf16(2, half, width))
    sends = call(
        functools.partial(halo_kernel, n),
        [halves, halves] + [end, end] * (half > WINDOW), [], 0, *held(crit),
    )
    kv_late, qg_early = sends[:2]
    kv_send, qg_send = sends[-2:]
    forward = [(i, i + 1) for i in range(chunks - 1)]
    backward = [(i + 1, i) for i in range(chunks - 1)]
    kv_halo = lax.ppermute(kv_send, "chunk", forward)
    qg_halo = lax.ppermute(qg_send, "chunk", backward)
    rest = exchanged(REST_ORDER, packed((0, 1), (2, 3)))
    stat_out = vmem(f32(-(-3 * heads // 8) * 8, WINDOW))
    qg_late, kv_early, dq_late, partial = call(
        functools.partial(late_kernel, n, heads),
        [halves, halves, vmem(bf16(done, width)), vmem(f32(2, total, width))],
        [], 0,
        *held(rest), (kv_late,), (qg_early,), flops=LATE_FLOPS,
    )
    *dq, front, stat = call(
        functools.partial(early_kernel, n, heads),
        [vmem(bf16(2, rows, width))] * (n // 2) + [end, stat_out],
        [vmem(bf16(total, width)), vmem(f32(2, WINDOW, width))], 0,
        *held((qg_early, qg_late, kv_early, kv_late, kv_halo, dq_late, partial)),
    )
    stat_halo = lax.ppermute(stat, "chunk", backward)
    dq = exchanged(DQ_ORDER, dq, 2)
    other, = call(
        core_kernel, [vmem(bf16(n // 2, rows, width))], [], 0, *held(dq)
    )
    other = lax.ppermute(other, GROUP, [(i, i ^ 1) for i in range(n)])
    dkv = call(
        functools.partial(edge_kernel, n, heads),
        [vmem(piece)] * n, [vmem(bf16(2, total, width)), vmem(f32(2, done, width))], 0,
        *held((kv_early, kv_late, qg_halo, front, partial, stat_halo)), flops=EDGE_FLOPS,
    )
    dkv = exchanged(DKV_ORDER, dkv)
    out = bf16(rows, model)
    return tuple(
        call(functools.partial(unpack_kernel, n), [out] * 3, [], 3 * n, *held(dq), (other,), *held(dkv))
    )


def solution(mesh):
    seq, head = mesh.devices.shape
    part = max(1, min(seq, HEADS // 2 // head))
    fine = Mesh(mesh.devices.reshape(seq // part, part, head), AXES)
    placed = P(AXES, None)
    return jax.shard_map(
        per_device,
        mesh=fine,
        in_specs=(placed,) * 4,
        out_specs=(placed,) * 3,
        check_vma=False,
    )
```

```python
import functools
import math

import jax
import jax.numpy as jnp
from jax import lax
from jax.experimental import pallas as pl
from jax.experimental.pallas import tpu as pltpu
from jax.sharding import Mesh, PartitionSpec as P

HEADS = 16
HEAD_DIM = 128
WINDOW = 512
TILE = 256
HALF = 128
AXES = ("chunk", "part", "head")
GROUP = ("part", "head")
SCALE = HEAD_DIM ** (-0.5)
SCALE_LOG2 = SCALE * math.log2(math.e)
MASKED = -1e30
VMEM_LIMIT = 48 * 1024 * 1024
NT = ((1,), (1,))
NN = ((1,), (0,))
CRIT_ORDER = (0, 6, 7, 2, 4, 1, 3, 5)
REST_ORDER = (0, 3, 5, 1, 6, 7, 2, 4)
DQ_ORDER = (0, 2, 1, 3)
DKV_ORDER = (0, 7, 3, 4, 6, 2, 5, 1)
DEPTH = 2
EDGE_FLOPS = 4000000000
LATE_FLOPS = 4000000000


def bf16(*shape):
    return jax.ShapeDtypeStruct(shape, jnp.bfloat16)


def f32(*shape):
    return jax.ShapeDtypeStruct(shape, jnp.float32)


def group_index():
    return lax.axis_index("part") * lax.axis_size("head") + lax.axis_index("head")


def group_size():
    return lax.axis_size("part") * lax.axis_size("head")


def aligned(index, step):
    return pl.multiple_of(index * step, step)


def copy_all(pairs, sems):
    copies = [pltpu.make_async_copy(src, dst, sems.at[i]) for i, (src, dst) in enumerate(pairs)]
    for copy in copies:
        copy.start()
    for copy in copies:
        copy.wait()


def dot(a, b, dims):
    return lax.dot_general(a, b, (dims, ((), ())), preferred_element_type=jnp.float32)


def pack_kernel(n, late_pair, early_pair, *refs):
    out = refs[4 : 4 + n]
    stage, sems = refs[4 + n :]
    me = group_index()
    width = stage.shape[2] // n

    def run(pair):
        loads = [
            pltpu.make_async_copy(refs[source], stage.at[t], sems.at[t])
            for t, source in enumerate(pair)
        ]
        for load in loads:
            load.start()
        for t, load in enumerate(loads):
            load.wait()
            for m in range(n):
                cols = pl.ds(aligned(jnp.bitwise_xor(me, m), width), width)
                out[m][t] = stage[t, :, cols]

    @pl.when(me >= n // 2)
    def _():
        run(late_pair)

    @pl.when(me < n // 2)
    def _():
        run(early_pair)


def place_all(pieces, late, early, me):
    n = len(pieces)
    rows = pieces[0].shape[1]

    def run(near, far):
        for m in range(n):
            at = pl.ds(aligned(jnp.bitwise_and(jnp.bitwise_xor(me, m), n // 2 - 1), rows), rows)
            (near if m < n // 2 else far)[:, at] = pieces[m][...]

    @pl.when(me >= n // 2)
    def _():
        run(late, early)

    @pl.when(me < n // 2)
    def _():
        run(early, late)


def halo_kernel(n, *refs):
    crit = by_slot(CRIT_ORDER, refs[:n])
    kv_late, qg_early, *sends = refs[n:]
    place_all(crit, kv_late, qg_early, group_index())
    if sends:
        sends[0][...] = kv_late[:, kv_late.shape[1] - WINDOW :]
        sends[1][...] = qg_early[:, :WINDOW]


def load(parts, t, lo, hi, lanes):
    out, start = [], 0
    for ref in parts:
        a, b = max(lo - start, 0), min(hi - start, ref.shape[1])
        if a < b:
            out.append(ref[t, a:b, lanes])
        start += ref.shape[1]
    return out[0] if len(out) == 1 else jnp.concatenate(out, axis=0)


def softmax_block(s, dp, bias, blind):
    row = lax.broadcasted_iota(jnp.int32, (HALF, HALF), 0)
    col = lax.broadcasted_iota(jnp.int32, (HALF, HALF), 1)
    span = WINDOW // HALF + 1
    nothing = jnp.zeros((HALF, HALF), jnp.bfloat16)
    p_parts, ds_parts, stats = [], [], []
    for c in range(TILE // HALF):
        cols = slice(c * HALF, (c + 1) * HALF)
        parts = [s[(c + r) * HALF : (c + r + 1) * HALF, cols] for r in range(span)]
        parts[0] = jnp.where(row > col, parts[0], MASKED)
        parts[-1] = jnp.where(row <= col, parts[-1], MASKED)
        parts = [b + bias if (c + r) * HALF < blind else b for r, b in enumerate(parts)]
        sc = jnp.concatenate(parts, axis=0)
        dpc = dp[c * HALF : (c + span) * HALF, cols]
        top = jnp.max(sc, axis=0, keepdims=True) * SCALE_LOG2
        e = jnp.exp2(sc * SCALE_LOG2 - top)
        inverse = 1.0 / jnp.sum(e, axis=0, keepdims=True)
        p = e * inverse
        dots = jnp.sum(p * dpc, axis=0, keepdims=True)
        ds = (p * (dpc - dots)).astype(jnp.bfloat16)
        pad = [nothing] * c, [nothing] * (TILE // HALF - 1 - c)
        p_parts.append(jnp.concatenate([*pad[0], p.astype(jnp.bfloat16), *pad[1]], axis=0))
        ds_parts.append(jnp.concatenate([*pad[0], ds, *pad[1]], axis=0))
        stats.append((top, inverse, dots))
    return jnp.concatenate(p_parts, axis=1), jnp.concatenate(ds_parts, axis=1), stats


def staged(blocks, first, second, third):
    made, held_back = {}, {}
    for i in range(len(blocks) + DEPTH):
        if i < len(blocks):
            made[i] = first(*blocks[i])
        j = i - DEPTH // 2
        if 0 <= j < len(blocks):
            held_back[j] = second(*blocks[j], *made.pop(j))
        k = i - DEPTH
        if 0 <= k < len(blocks):
            third(*blocks[k], *held_back.pop(k))


def late_kernel(n, heads, *refs):
    rest = by_slot(REST_ORDER, refs[:n])
    kv_late, qg_early, qg_late, kv_early, dq, dkv = refs[n:]
    place_all(rest, qg_late, kv_early, group_index())
    total = dkv.shape[1]
    qg, kv = (qg_early, qg_late), (kv_early, kv_late)
    blocks = [(h, start) for h in range(heads) for start in range(0, total - WINDOW, TILE)]
    lanes_of = [slice(h * HEAD_DIM, (h + 1) * HEAD_DIM) for h in range(heads)]
    key_ts = [load(kv, 0, 0, total, lanes).T for lanes in lanes_of]

    def products(h, start):
        qb, gb = (load(qg, t, start + WINDOW, start + WINDOW + TILE, lanes_of[h]) for t in range(2))
        kb, vb = (load(kv, t, start, start + 3 * TILE, lanes_of[h]) for t in range(2))
        return dot(kb, qb, NT), dot(vb, gb, NT)

    def gradients(h, start, p_low, ds):
        lanes = lanes_of[h]
        keys = slice(start, start + 3 * TILE)
        mine = slice(start + WINDOW, start + WINDOW + TILE)
        qb, gb = (load(qg, t, start + WINDOW, start + WINDOW + TILE, lanes) for t in range(2))
        dq[slice(start, start + TILE), lanes] = (
            (dot(key_ts[h][:, keys], ds, NN) * SCALE).astype(jnp.bfloat16).T
        )
        for t, add in enumerate((dot(ds, qb, NN), dot(p_low, gb, NN))):
            if start == 0:
                dkv[t, keys, lanes] = add
            else:
                older = slice(start, start + 2 * TILE)
                dkv[t, older, lanes] += add[: 2 * TILE]
                dkv[t, mine, lanes] = add[2 * TILE :]

    staged(blocks, products, lambda h, start, s, dp: softmax_block(s, dp, 0.0, 0)[:2], gradients)


def early_kernel(n, heads, *refs):
    qg_early, qg_late, kv_early, kv_late, kv_halo, dq_in, dkv_in = refs[:7]
    refs = refs[7:]
    dq_out = refs[: n // 2]
    front, stat, dq, acc = refs[n // 2 :]
    me = group_index()
    rows = dq_out[0].shape[1]
    first = lax.axis_index("chunk") == 0
    stat[...] = jnp.zeros_like(stat)
    dq[WINDOW:] = dq_in[...]
    acc[...] = dkv_in[:, :WINDOW]
    bias = jnp.where(first, MASKED, 0.0)
    qg, kv = (qg_early, qg_late), (kv_halo, kv_early, kv_late)
    blocks = [(h, start) for h in range(heads) for start in range(0, WINDOW, TILE)]
    lanes_of = [slice(h * HEAD_DIM, (h + 1) * HEAD_DIM) for h in range(heads)]
    key_ts = [load(kv, 0, 0, 2 * WINDOW, lanes).T for lanes in lanes_of]

    def products(h, start):
        qb, gb = (load(qg, t, start, start + TILE, lanes_of[h]) for t in range(2))
        kb, vb = (load(kv, t, start, start + 3 * TILE, lanes_of[h]) for t in range(2))
        return dot(kb, qb, NT), dot(vb, gb, NT)

    def probabilities(h, start, s, dp):
        p_low, ds, stats = softmax_block(s, dp, bias, WINDOW - start)
        for c, rows_of in enumerate(stats):
            at = slice(start + c * HALF, start + (c + 1) * HALF)
            for k, value in enumerate(rows_of):
                stat[3 * h + k : 3 * h + k + 1, at] = value
        return p_low, ds

    def gradients(h, start, p_low, ds):
        lanes = lanes_of[h]
        keys = slice(start, start + 3 * TILE)
        qb, gb = (load(qg, t, start, start + TILE, lanes) for t in range(2))
        dq[slice(start, start + TILE), lanes] = (
            (dot(key_ts[h][:, keys], ds, NN) * SCALE).astype(jnp.bfloat16).T
        )
        own = slice(0, start + TILE)
        acc[0, own, lanes] += dot(ds[WINDOW - start :], qb, NN)
        acc[1, own, lanes] += dot(p_low[WINDOW - start :], gb, NN)

    staged(blocks, products, probabilities, gradients)
    for m in range(n):
        dq_out[m // 2][m % 2] = dq[pl.ds(aligned(jnp.bitwise_xor(me, m), rows), rows)]
    front[0] = (acc[0] * SCALE).astype(jnp.bfloat16)
    front[1] = acc[1].astype(jnp.bfloat16)


def edge_kernel(n, heads, *refs):
    kv_early, kv_late, qg, front, dkv_in, stat = refs[:6]
    refs = refs[6:]
    out = refs[:n]
    full, acc = refs[n:]
    me = group_index()
    total = dkv_in.shape[1]
    done = total - WINDOW
    rows = total // n
    kv = (kv_early, kv_late)
    row = lax.broadcasted_iota(jnp.int32, (TILE, TILE), 0)
    col = lax.broadcasted_iota(jnp.int32, (TILE, TILE), 1)
    acc[...] = dkv_in[:, WINDOW:]
    blocks = [(h, start) for h in range(heads) for start in range(0, WINDOW, TILE)]
    lanes_of = [slice(h * HEAD_DIM, (h + 1) * HEAD_DIM) for h in range(heads)]

    def products(h, start):
        mine = slice(start, start + TILE)
        kb, vb = (load(kv, t, done + start, total, lanes_of[h]) for t in range(2))
        return dot(kb, qg[0, mine, lanes_of[h]], NT), dot(vb, qg[1, mine, lanes_of[h]], NT)

    def probabilities(h, start, s, dp):
        mine = slice(start, start + TILE)
        newest = jnp.where(row > col, s[:TILE], MASKED)
        s = newest if len(s) == TILE else jnp.concatenate([newest, s[TILE:]], axis=0)
        top, inverse, dots = (stat[3 * h + k : 3 * h + k + 1, mine] for k in range(3))
        p = jnp.exp2(s * SCALE_LOG2 - top) * inverse
        return p.astype(jnp.bfloat16), (p * (dp - dots)).astype(jnp.bfloat16)

    def gradients(h, start, p_low, ds):
        mine = slice(start, start + TILE)
        at = slice(done - WINDOW + start, done)
        acc[0, at, lanes_of[h]] += dot(ds, qg[0, mine, lanes_of[h]], NN)
        acc[1, at, lanes_of[h]] += dot(p_low, qg[1, mine, lanes_of[h]], NN)

    staged(blocks, products, probabilities, gradients)
    full[:, :WINDOW] = front[...]
    full[0, WINDOW:] = (acc[0] * SCALE).astype(jnp.bfloat16)
    full[1, WINDOW:] = acc[1].astype(jnp.bfloat16)
    for m in range(n):
        out[m][...] = full[:, pl.ds(aligned(jnp.bitwise_xor(me, m), rows), rows)]


def core_kernel(*refs):
    *pieces, out = refs
    for slot, piece in enumerate(by_slot(DQ_ORDER, pieces)):
        out[slot] = piece[1]


def unpack_kernel(n, *refs):
    chips = n // 2
    dq_in = by_slot(DQ_ORDER, refs[:chips])
    other = refs[chips]
    dkv_in = by_slot(DKV_ORDER, refs[chips + 1 : chips + 1 + n])
    dq, dk, dv, sems = refs[chips + 1 + n :]
    me = group_index()
    width = other.shape[2]
    pairs = []
    for m in range(n):
        cols = pl.ds(aligned(jnp.bitwise_xor(me, m), width), width)
        pairs.append((other.at[m // 2] if m % 2 else dq_in[m // 2].at[0], dq.at[:, cols]))
        pairs.append((dkv_in[m].at[0], dk.at[:, cols]))
        pairs.append((dkv_in[m].at[1], dv.at[:, cols]))
    copy_all(pairs, sems)


def call(kernel, outs, scratch, sems, *operands, space=pl.ANY, limit=VMEM_LIMIT, flops=0):
    held = pl.BlockSpec(memory_space=pltpu.VMEM)
    loose = pl.BlockSpec(memory_space=space)
    arrays = [x[0] if isinstance(x, tuple) else x for x in operands]
    return pl.pallas_call(
        kernel,
        out_shape=outs,
        in_specs=[held if isinstance(x, tuple) else loose for x in operands],
        out_specs=[held if not isinstance(x, jax.ShapeDtypeStruct) else pl.BlockSpec(memory_space=pl.ANY) for x in outs],
        scratch_shapes=[*scratch, *([pltpu.SemaphoreType.DMA((sems,))] if sems else [])],
        compiler_params=pltpu.CompilerParams(vmem_limit_bytes=limit),
        cost_estimate=pl.CostEstimate(flops=flops, bytes_accessed=0, transcendentals=0) if flops else None,
    )(*arrays)


def held(arrays):
    return [(x,) for x in arrays]


def vmem(shape):
    return pltpu.VMEM(shape.shape, shape.dtype)


def order_of(order, n):
    return [m for m in order if m < n] + list(range(len(order), n))


def by_slot(order, refs):
    order = order_of(order, len(refs))
    return [refs[order.index(m)] for m in range(len(refs))]


def exchanged(order, pieces, step=1):
    n = len(pieces)
    return [
        lax.ppermute(pieces[m], GROUP, [(i, i ^ (step * m)) for i in range(step * n)]) if m else pieces[0]
        for m in order_of(order, n)
    ]


def per_device(queries, key_vectors, value_vectors, grad_output):
    n = group_size()
    chunks = lax.axis_size("chunk")
    rows, model = queries.shape
    heads = HEADS // n
    width = model // n
    total = n * rows
    done = total - WINDOW
    piece = bf16(2, rows, width)
    arguments = (queries, grad_output, key_vectors, value_vectors)

    def packed(late_pair, early_pair):
        return call(
            functools.partial(pack_kernel, n, late_pair, early_pair), [vmem(piece)] * n,
            [vmem(bf16(2, rows, model))], 2, *arguments, space=pltpu.HBM, limit=None,
        )

    crit = exchanged(CRIT_ORDER, packed((2, 3), (0, 1)))
    half = total // 2
    end = vmem(bf16(2, WINDOW, width))
    halves = vmem(bf16(2, half, width))
    sends = call(
        functools.partial(halo_kernel, n),
        [halves, halves] + [end, end] * (half > WINDOW), [], 0, *held(crit),
    )
    kv_late, qg_early = sends[:2]
    kv_send, qg_send = sends[-2:]
    forward = [(i, i + 1) for i in range(chunks - 1)]
    backward = [(i + 1, i) for i in range(chunks - 1)]
    kv_halo = lax.ppermute(kv_send, "chunk", forward)
    qg_halo = lax.ppermute(qg_send, "chunk", backward)
    rest = exchanged(REST_ORDER, packed((0, 1), (2, 3)))
    stat_out = vmem(f32(-(-3 * heads // 8) * 8, WINDOW))
    qg_late, kv_early, dq_late, partial = call(
        functools.partial(late_kernel, n, heads),
        [halves, halves, vmem(bf16(done, width)), vmem(f32(2, total, width))],
        [], 0,
        *held(rest), (kv_late,), (qg_early,), flops=LATE_FLOPS,
    )
    *dq, front, stat = call(
        functools.partial(early_kernel, n, heads),
        [vmem(bf16(2, rows, width))] * (n // 2) + [end, stat_out],
        [vmem(bf16(total, width)), vmem(f32(2, WINDOW, width))], 0,
        *held((qg_early, qg_late, kv_early, kv_late, kv_halo, dq_late, partial)),
    )
    stat_halo = lax.ppermute(stat, "chunk", backward)
    dq = exchanged(DQ_ORDER, dq, 2)
    other, = call(
        core_kernel, [vmem(bf16(n // 2, rows, width))], [], 0, *held(dq)
    )
    other = lax.ppermute(other, GROUP, [(i, i ^ 1) for i in range(n)])
    dkv = call(
        functools.partial(edge_kernel, n, heads),
        [vmem(piece)] * n, [vmem(bf16(2, total, width)), vmem(f32(2, done, width))], 0,
        *held((kv_early, kv_late, qg_halo, front, partial, stat_halo)), flops=EDGE_FLOPS,
    )
    dkv = exchanged(DKV_ORDER, dkv)
    out = bf16(rows, model)
    return tuple(
        call(functools.partial(unpack_kernel, n), [out] * 3, [], 3 * n, *held(dq), (other,), *held(dkv))
    )


def solution(mesh):
    seq, head = mesh.devices.shape
    part = max(1, min(seq, HEADS // 2 // head))
    fine = Mesh(mesh.devices.reshape(seq // part, part, head), AXES)
    placed = P(AXES, None)
    return jax.shard_map(
        per_device,
        mesh=fine,
        in_specs=(placed,) * 4,
        out_specs=(placed,) * 3,
        check_vma=False,
    )
```

```python
import functools
import math

import jax
import jax.numpy as jnp
from jax import lax
from jax.experimental import pallas as pl
from jax.experimental.pallas import tpu as pltpu
from jax.sharding import Mesh, PartitionSpec as P

HEADS = 16
HEAD_DIM = 128
WINDOW = 512
TILE = 256
HALF = 128
AXES = ("chunk", "part", "head")
GROUP = ("part", "head")
SCALE = HEAD_DIM ** (-0.5)
SCALE_LOG2 = SCALE * math.log2(math.e)
MASKED = -1e30
VMEM_LIMIT = 48 * 1024 * 1024
NT = ((1,), (1,))
NN = ((1,), (0,))
CRIT_ORDER = (0, 6, 7, 2, 4, 1, 3, 5)
REST_ORDER = (0, 3, 5, 1, 6, 7, 2, 4)
DQ_ORDER = (0, 2, 1, 3)
DKV_ORDER = (0, 7, 3, 4, 6, 2, 5, 1)
DEPTH = 2
EDGE_FLOPS = 4000000000
LATE_FLOPS = 4000000000


def bf16(*shape):
    return jax.ShapeDtypeStruct(shape, jnp.bfloat16)


def f32(*shape):
    return jax.ShapeDtypeStruct(shape, jnp.float32)


def group_index():
    return lax.axis_index("part") * lax.axis_size("head") + lax.axis_index("head")


def group_size():
    return lax.axis_size("part") * lax.axis_size("head")


def aligned(index, step):
    return pl.multiple_of(index * step, step)


def copy_all(pairs, sems):
    copies = [pltpu.make_async_copy(src, dst, sems.at[i]) for i, (src, dst) in enumerate(pairs)]
    for copy in copies:
        copy.start()
    for copy in copies:
        copy.wait()


def dot(a, b, dims):
    return lax.dot_general(a, b, (dims, ((), ())), preferred_element_type=jnp.float32)


def pack_kernel(n, late_pair, early_pair, *refs):
    out = refs[4 : 4 + n]
    stage, sems = refs[4 + n :]
    me = group_index()
    width = stage.shape[2] // n

    def run(pair):
        loads = [
            pltpu.make_async_copy(refs[source], stage.at[t], sems.at[t])
            for t, source in enumerate(pair)
        ]
        for load in loads:
            load.start()
        for t, load in enumerate(loads):
            load.wait()
            for m in range(n):
                cols = pl.ds(aligned(jnp.bitwise_xor(me, m), width), width)
                out[m][t] = stage[t, :, cols]

    @pl.when(me >= n // 2)
    def _():
        run(late_pair)

    @pl.when(me < n // 2)
    def _():
        run(early_pair)


def place_all(pieces, late, early, me):
    n = len(pieces)
    rows = pieces[0].shape[1]

    def run(near, far):
        for m in range(n):
            at = pl.ds(aligned(jnp.bitwise_and(jnp.bitwise_xor(me, m), n // 2 - 1), rows), rows)
            (near if m < n // 2 else far)[:, at] = pieces[m][...]

    @pl.when(me >= n // 2)
    def _():
        run(late, early)

    @pl.when(me < n // 2)
    def _():
        run(early, late)


def halo_kernel(n, *refs):
    crit = by_slot(CRIT_ORDER, refs[:n])
    kv_late, qg_early, *sends = refs[n:]
    place_all(crit, kv_late, qg_early, group_index())
    if sends:
        sends[0][...] = kv_late[:, kv_late.shape[1] - WINDOW :]
        sends[1][...] = qg_early[:, :WINDOW]


def load(parts, t, lo, hi, lanes):
    out, start = [], 0
    for ref in parts:
        a, b = max(lo - start, 0), min(hi - start, ref.shape[1])
        if a < b:
            out.append(ref[t, a:b, lanes])
        start += ref.shape[1]
    return out[0] if len(out) == 1 else jnp.concatenate(out, axis=0)


def softmax_block(s, dp, bias, blind):
    row = lax.broadcasted_iota(jnp.int32, (HALF, HALF), 0)
    col = lax.broadcasted_iota(jnp.int32, (HALF, HALF), 1)
    span = WINDOW // HALF + 1
    nothing = jnp.zeros((HALF, HALF), jnp.bfloat16)
    p_parts, ds_parts, stats = [], [], []
    for c in range(TILE // HALF):
        cols = slice(c * HALF, (c + 1) * HALF)
        parts = [s[(c + r) * HALF : (c + r + 1) * HALF, cols] for r in range(span)]
        parts[0] = jnp.where(row > col, parts[0], MASKED)
        parts[-1] = jnp.where(row <= col, parts[-1], MASKED)
        parts = [b + bias if (c + r) * HALF < blind else b for r, b in enumerate(parts)]
        sc = jnp.concatenate(parts, axis=0)
        dpc = dp[c * HALF : (c + span) * HALF, cols]
        top = jnp.max(sc, axis=0, keepdims=True) * SCALE_LOG2
        e = jnp.exp2(sc * SCALE_LOG2 - top)
        inverse = 1.0 / jnp.sum(e, axis=0, keepdims=True)
        p = e * inverse
        dots = jnp.sum(p * dpc, axis=0, keepdims=True)
        ds = (p * (dpc - dots)).astype(jnp.bfloat16)
        pad = [nothing] * c, [nothing] * (TILE // HALF - 1 - c)
        p_parts.append(jnp.concatenate([*pad[0], p.astype(jnp.bfloat16), *pad[1]], axis=0))
        ds_parts.append(jnp.concatenate([*pad[0], ds, *pad[1]], axis=0))
        stats.append((top, inverse, dots))
    return jnp.concatenate(p_parts, axis=1), jnp.concatenate(ds_parts, axis=1), stats


def staged(blocks, first, second, third):
    made, held_back = {}, {}
    for i in range(len(blocks) + DEPTH):
        if i < len(blocks):
            made[i] = first(*blocks[i])
        j = i - DEPTH // 2
        if 0 <= j < len(blocks):
            held_back[j] = second(*blocks[j], *made.pop(j))
        k = i - DEPTH
        if 0 <= k < len(blocks):
            third(*blocks[k], *held_back.pop(k))


def late_kernel(n, heads, *refs):
    rest = by_slot(REST_ORDER, refs[:n])
    kv_late, qg_early, qg_late, kv_early, dq, dkv, turned = refs[n:]
    place_all(rest, qg_late, kv_early, group_index())
    total = dkv.shape[1]
    qg, kv = (qg_early, qg_late), (kv_early, kv_late)
    blocks = [(h, start) for h in range(heads) for start in range(0, total - WINDOW, TILE)]
    lanes_of = [slice(h * HEAD_DIM, (h + 1) * HEAD_DIM) for h in range(heads)]
    key_ts = [load(kv, 0, 0, total, lanes).T for lanes in lanes_of]
    for h in range(heads):
        turned[h] = key_ts[h][:, :WINDOW]

    def products(h, start):
        qb, gb = (load(qg, t, start + WINDOW, start + WINDOW + TILE, lanes_of[h]) for t in range(2))
        kb, vb = (load(kv, t, start, start + 3 * TILE, lanes_of[h]) for t in range(2))
        return dot(kb, qb, NT), dot(vb, gb, NT)

    def gradients(h, start, p_low, ds):
        lanes = lanes_of[h]
        keys = slice(start, start + 3 * TILE)
        mine = slice(start + WINDOW, start + WINDOW + TILE)
        qb, gb = (load(qg, t, start + WINDOW, start + WINDOW + TILE, lanes) for t in range(2))
        dq[slice(start, start + TILE), lanes] = (
            (dot(key_ts[h][:, keys], ds, NN) * SCALE).astype(jnp.bfloat16).T
        )
        for t, add in enumerate((dot(ds, qb, NN), dot(p_low, gb, NN))):
            if start == 0:
                dkv[t, keys, lanes] = add
            else:
                older = slice(start, start + 2 * TILE)
                dkv[t, older, lanes] += add[: 2 * TILE]
                dkv[t, mine, lanes] = add[2 * TILE :]

    staged(blocks, products, lambda h, start, s, dp: softmax_block(s, dp, 0.0, 0)[:2], gradients)


def early_kernel(n, heads, *refs):
    qg_early, qg_late, kv_early, kv_late, kv_halo, dq_in, dkv_in, turned = refs[:8]
    refs = refs[8:]
    dq_out = refs[: n // 2]
    front, stat, dq, acc = refs[n // 2 :]
    me = group_index()
    rows = dq_out[0].shape[1]
    first = lax.axis_index("chunk") == 0
    stat[...] = jnp.zeros_like(stat)
    dq[WINDOW:] = dq_in[...]
    acc[...] = dkv_in[:, :WINDOW]
    bias = jnp.where(first, MASKED, 0.0)
    qg, kv = (qg_early, qg_late), (kv_halo, kv_early, kv_late)
    blocks = [(h, start) for h in range(heads) for start in range(0, WINDOW, TILE)]
    lanes_of = [slice(h * HEAD_DIM, (h + 1) * HEAD_DIM) for h in range(heads)]
    key_ts = [
        jnp.concatenate([kv_halo[0, :, lanes].T, turned[h]], axis=1)
        for h, lanes in enumerate(lanes_of)
    ]

    def products(h, start):
        qb, gb = (load(qg, t, start, start + TILE, lanes_of[h]) for t in range(2))
        kb, vb = (load(kv, t, start, start + 3 * TILE, lanes_of[h]) for t in range(2))
        return dot(kb, qb, NT), dot(vb, gb, NT)

    def probabilities(h, start, s, dp):
        p_low, ds, stats = softmax_block(s, dp, bias, WINDOW - start)
        for c, rows_of in enumerate(stats):
            at = slice(start + c * HALF, start + (c + 1) * HALF)
            for k, value in enumerate(rows_of):
                stat[3 * h + k : 3 * h + k + 1, at] = value
        return p_low, ds

    def gradients(h, start, p_low, ds):
        lanes = lanes_of[h]
        keys = slice(start, start + 3 * TILE)
        qb, gb = (load(qg, t, start, start + TILE, lanes) for t in range(2))
        dq[slice(start, start + TILE), lanes] = (
            (dot(key_ts[h][:, keys], ds, NN) * SCALE).astype(jnp.bfloat16).T
        )
        own = slice(0, start + TILE)
        acc[0, own, lanes] += dot(ds[WINDOW - start :], qb, NN)
        acc[1, own, lanes] += dot(p_low[WINDOW - start :], gb, NN)

    staged(blocks, products, probabilities, gradients)
    for m in range(n):
        dq_out[m // 2][m % 2] = dq[pl.ds(aligned(jnp.bitwise_xor(me, m), rows), rows)]
    front[0] = (acc[0] * SCALE).astype(jnp.bfloat16)
    front[1] = acc[1].astype(jnp.bfloat16)


def edge_kernel(n, heads, *refs):
    kv_early, kv_late, qg, front, dkv_in, stat = refs[:6]
    refs = refs[6:]
    out = refs[:n]
    full, acc = refs[n:]
    me = group_index()
    total = dkv_in.shape[1]
    done = total - WINDOW
    rows = total // n
    kv = (kv_early, kv_late)
    row = lax.broadcasted_iota(jnp.int32, (TILE, TILE), 0)
    col = lax.broadcasted_iota(jnp.int32, (TILE, TILE), 1)
    acc[...] = dkv_in[:, WINDOW:]
    blocks = [(h, start) for h in range(heads) for start in range(0, WINDOW, TILE)]
    lanes_of = [slice(h * HEAD_DIM, (h + 1) * HEAD_DIM) for h in range(heads)]

    def products(h, start):
        mine = slice(start, start + TILE)
        kb, vb = (load(kv, t, done + start, total, lanes_of[h]) for t in range(2))
        return dot(kb, qg[0, mine, lanes_of[h]], NT), dot(vb, qg[1, mine, lanes_of[h]], NT)

    def probabilities(h, start, s, dp):
        mine = slice(start, start + TILE)
        newest = jnp.where(row > col, s[:TILE], MASKED)
        s = newest if len(s) == TILE else jnp.concatenate([newest, s[TILE:]], axis=0)
        top, inverse, dots = (stat[3 * h + k : 3 * h + k + 1, mine] for k in range(3))
        p = jnp.exp2(s * SCALE_LOG2 - top) * inverse
        return p.astype(jnp.bfloat16), (p * (dp - dots)).astype(jnp.bfloat16)

    def gradients(h, start, p_low, ds):
        mine = slice(start, start + TILE)
        at = slice(done - WINDOW + start, done)
        acc[0, at, lanes_of[h]] += dot(ds, qg[0, mine, lanes_of[h]], NN)
        acc[1, at, lanes_of[h]] += dot(p_low, qg[1, mine, lanes_of[h]], NN)

    staged(blocks, products, probabilities, gradients)
    full[:, :WINDOW] = front[...]
    full[0, WINDOW:] = (acc[0] * SCALE).astype(jnp.bfloat16)
    full[1, WINDOW:] = acc[1].astype(jnp.bfloat16)
    for m in range(n):
        out[m][...] = full[:, pl.ds(aligned(jnp.bitwise_xor(me, m), rows), rows)]


def core_kernel(*refs):
    *pieces, out = refs
    for slot, piece in enumerate(by_slot(DQ_ORDER, pieces)):
        out[slot] = piece[1]


def unpack_kernel(n, *refs):
    chips = n // 2
    dq_in = by_slot(DQ_ORDER, refs[:chips])
    other = refs[chips]
    dkv_in = by_slot(DKV_ORDER, refs[chips + 1 : chips + 1 + n])
    dq, dk, dv, sems = refs[chips + 1 + n :]
    me = group_index()
    width = other.shape[2]
    pairs = []
    for m in range(n):
        cols = pl.ds(aligned(jnp.bitwise_xor(me, m), width), width)
        pairs.append((other.at[m // 2] if m % 2 else dq_in[m // 2].at[0], dq.at[:, cols]))
        pairs.append((dkv_in[m].at[0], dk.at[:, cols]))
        pairs.append((dkv_in[m].at[1], dv.at[:, cols]))
    copy_all(pairs, sems)


def call(kernel, outs, scratch, sems, *operands, space=pl.ANY, limit=VMEM_LIMIT, flops=0):
    held = pl.BlockSpec(memory_space=pltpu.VMEM)
    loose = pl.BlockSpec(memory_space=space)
    arrays = [x[0] if isinstance(x, tuple) else x for x in operands]
    return pl.pallas_call(
        kernel,
        out_shape=outs,
        in_specs=[held if isinstance(x, tuple) else loose for x in operands],
        out_specs=[held if not isinstance(x, jax.ShapeDtypeStruct) else pl.BlockSpec(memory_space=pl.ANY) for x in outs],
        scratch_shapes=[*scratch, *([pltpu.SemaphoreType.DMA((sems,))] if sems else [])],
        compiler_params=pltpu.CompilerParams(vmem_limit_bytes=limit),
        cost_estimate=pl.CostEstimate(flops=flops, bytes_accessed=0, transcendentals=0) if flops else None,
    )(*arrays)


def held(arrays):
    return [(x,) for x in arrays]


def vmem(shape):
    return pltpu.VMEM(shape.shape, shape.dtype)


def order_of(order, n):
    return [m for m in order if m < n] + list(range(len(order), n))


def by_slot(order, refs):
    order = order_of(order, len(refs))
    return [refs[order.index(m)] for m in range(len(refs))]


def exchanged(order, pieces, step=1):
    n = len(pieces)
    return [
        lax.ppermute(pieces[m], GROUP, [(i, i ^ (step * m)) for i in range(step * n)]) if m else pieces[0]
        for m in order_of(order, n)
    ]


def per_device(queries, key_vectors, value_vectors, grad_output):
    n = group_size()
    chunks = lax.axis_size("chunk")
    rows, model = queries.shape
    heads = HEADS // n
    width = model // n
    total = n * rows
    done = total - WINDOW
    piece = bf16(2, rows, width)
    arguments = (queries, grad_output, key_vectors, value_vectors)

    def packed(late_pair, early_pair):
        return call(
            functools.partial(pack_kernel, n, late_pair, early_pair), [vmem(piece)] * n,
            [vmem(bf16(2, rows, model))], 2, *arguments, space=pltpu.HBM, limit=None,
        )

    crit = exchanged(CRIT_ORDER, packed((2, 3), (0, 1)))
    half = total // 2
    end = vmem(bf16(2, WINDOW, width))
    halves = vmem(bf16(2, half, width))
    sends = call(
        functools.partial(halo_kernel, n),
        [halves, halves] + [end, end] * (half > WINDOW), [], 0, *held(crit),
    )
    kv_late, qg_early = sends[:2]
    kv_send, qg_send = sends[-2:]
    forward = [(i, i + 1) for i in range(chunks - 1)]
    backward = [(i + 1, i) for i in range(chunks - 1)]
    kv_halo = lax.ppermute(kv_send, "chunk", forward)
    qg_halo = lax.ppermute(qg_send, "chunk", backward)
    rest = exchanged(REST_ORDER, packed((0, 1), (2, 3)))
    stat_out = vmem(f32(-(-3 * heads // 8) * 8, WINDOW))
    qg_late, kv_early, dq_late, partial, turned = call(
        functools.partial(late_kernel, n, heads),
        [
            halves, halves, vmem(bf16(done, width)), vmem(f32(2, total, width)),
            vmem(bf16(heads, HEAD_DIM, WINDOW)),
        ],
        [], 0,
        *held(rest), (kv_late,), (qg_early,), flops=LATE_FLOPS,
    )
    *dq, front, stat = call(
        functools.partial(early_kernel, n, heads),
        [vmem(bf16(2, rows, width))] * (n // 2) + [end, stat_out],
        [vmem(bf16(total, width)), vmem(f32(2, WINDOW, width))], 0,
        *held((qg_early, qg_late, kv_early, kv_late, kv_halo, dq_late, partial, turned)),
    )
    stat_halo = lax.ppermute(stat, "chunk", backward)
    dq = exchanged(DQ_ORDER, dq, 2)
    other, = call(
        core_kernel, [vmem(bf16(n // 2, rows, width))], [], 0, *held(dq)
    )
    other = lax.ppermute(other, GROUP, [(i, i ^ 1) for i in range(n)])
    dkv = call(
        functools.partial(edge_kernel, n, heads),
        [vmem(piece)] * n, [vmem(bf16(2, total, width)), vmem(f32(2, done, width))], 0,
        *held((kv_early, kv_late, qg_halo, front, partial, stat_halo)), flops=EDGE_FLOPS,
    )
    dkv = exchanged(DKV_ORDER, dkv)
    out = bf16(rows, model)
    return tuple(
        call(functools.partial(unpack_kernel, n), [out] * 3, [], 3 * n, *held(dq), (other,), *held(dkv))
    )


def solution(mesh):
    seq, head = mesh.devices.shape
    part = max(1, min(seq, HEADS // 2 // head))
    fine = Mesh(mesh.devices.reshape(seq // part, part, head), AXES)
    placed = P(AXES, None)
    return jax.shard_map(
        per_device,
        mesh=fine,
        in_specs=(placed,) * 4,
        out_specs=(placed,) * 3,
        check_vma=False,
    )
```

```python
import functools
import math

import jax
import jax.numpy as jnp
from jax import lax
from jax.experimental import pallas as pl
from jax.experimental.pallas import tpu as pltpu
from jax.sharding import Mesh, PartitionSpec as P

HEADS = 16
HEAD_DIM = 128
WINDOW = 512
TILE = 256
HALF = 128
AXES = ("chunk", "part", "head")
GROUP = ("part", "head")
SCALE = HEAD_DIM ** (-0.5)
SCALE_LOG2 = SCALE * math.log2(math.e)
MASKED = -1e30
VMEM_LIMIT = 28 * 1024 * 1024
NT = ((1,), (1,))
NN = ((1,), (0,))
CRIT_ORDER = (0, 6, 7, 2, 4, 1, 3, 5)
REST_ORDER = (0, 3, 5, 1, 6, 7, 2, 4)
DQ_ORDER = (0, 2, 1, 3)
DKV_ORDER = (0, 7, 3, 4, 6, 2, 5, 1)
DEPTH = 2
EDGE_FLOPS = 4000000000
LATE_FLOPS = 4000000000


def bf16(*shape):
    return jax.ShapeDtypeStruct(shape, jnp.bfloat16)


def f32(*shape):
    return jax.ShapeDtypeStruct(shape, jnp.float32)


def group_index():
    return lax.axis_index("part") * lax.axis_size("head") + lax.axis_index("head")


def group_size():
    return lax.axis_size("part") * lax.axis_size("head")


def aligned(index, step):
    return pl.multiple_of(index * step, step)


def copy_all(pairs, sems):
    copies = [pltpu.make_async_copy(src, dst, sems.at[i]) for i, (src, dst) in enumerate(pairs)]
    for copy in copies:
        copy.start()
    for copy in copies:
        copy.wait()


def dot(a, b, dims):
    return lax.dot_general(a, b, (dims, ((), ())), preferred_element_type=jnp.float32)


def pack_kernel(n, late_pair, early_pair, *refs):
    out = refs[4 : 4 + n]
    stage, sems = refs[4 + n :]
    me = group_index()
    width = stage.shape[2] // n

    def run(pair):
        loads = [
            pltpu.make_async_copy(refs[source], stage.at[t], sems.at[t])
            for t, source in enumerate(pair)
        ]
        for load in loads:
            load.start()
        for t, load in enumerate(loads):
            load.wait()
            for m in range(n):
                cols = pl.ds(aligned(jnp.bitwise_xor(me, m), width), width)
                out[m][t] = stage[t, :, cols]

    @pl.when(me >= n // 2)
    def _():
        run(late_pair)

    @pl.when(me < n // 2)
    def _():
        run(early_pair)


def place_all(pieces, late, early, me):
    n = len(pieces)
    rows = pieces[0].shape[1]

    def run(near, far):
        for m in range(n):
            at = pl.ds(aligned(jnp.bitwise_and(jnp.bitwise_xor(me, m), n // 2 - 1), rows), rows)
            (near if m < n // 2 else far)[:, at] = pieces[m][...]

    @pl.when(me >= n // 2)
    def _():
        run(late, early)

    @pl.when(me < n // 2)
    def _():
        run(early, late)


def halo_kernel(n, *refs):
    crit = by_slot(CRIT_ORDER, refs[:n])
    kv_late, qg_early, *sends = refs[n:]
    place_all(crit, kv_late, qg_early, group_index())
    if sends:
        sends[0][...] = kv_late[:, kv_late.shape[1] - WINDOW :]
        sends[1][...] = qg_early[:, :WINDOW]


def load(parts, t, lo, hi, lanes):
    out, start = [], 0
    for ref in parts:
        a, b = max(lo - start, 0), min(hi - start, ref.shape[1])
        if a < b:
            out.append(ref[t, a:b, lanes])
        start += ref.shape[1]
    return out[0] if len(out) == 1 else jnp.concatenate(out, axis=0)


def softmax_block(s, dp, bias, blind):
    row = lax.broadcasted_iota(jnp.int32, (HALF, HALF), 0)
    col = lax.broadcasted_iota(jnp.int32, (HALF, HALF), 1)
    span = WINDOW // HALF + 1
    nothing = jnp.zeros((HALF, HALF), jnp.bfloat16)
    p_parts, ds_parts, stats = [], [], []
    for c in range(TILE // HALF):
        cols = slice(c * HALF, (c + 1) * HALF)
        parts = [s[(c + r) * HALF : (c + r + 1) * HALF, cols] for r in range(span)]
        parts[0] = jnp.where(row > col, parts[0], MASKED)
        parts[-1] = jnp.where(row <= col, parts[-1], MASKED)
        parts = [b + bias if (c + r) * HALF < blind else b for r, b in enumerate(parts)]
        sc = jnp.concatenate(parts, axis=0)
        dpc = dp[c * HALF : (c + span) * HALF, cols]
        top = jnp.max(sc, axis=0, keepdims=True) * SCALE_LOG2
        e = jnp.exp2(sc * SCALE_LOG2 - top)
        inverse = 1.0 / jnp.sum(e, axis=0, keepdims=True)
        p = e * inverse
        dots = jnp.sum(p * dpc, axis=0, keepdims=True)
        ds = (p * (dpc - dots)).astype(jnp.bfloat16)
        pad = [nothing] * c, [nothing] * (TILE // HALF - 1 - c)
        p_parts.append(jnp.concatenate([*pad[0], p.astype(jnp.bfloat16), *pad[1]], axis=0))
        ds_parts.append(jnp.concatenate([*pad[0], ds, *pad[1]], axis=0))
        stats.append((top, inverse, dots))
    return jnp.concatenate(p_parts, axis=1), jnp.concatenate(ds_parts, axis=1), stats


def staged(blocks, first, second, third):
    made, held_back = {}, {}
    for i in range(len(blocks) + DEPTH):
        if i < len(blocks):
            made[i] = first(*blocks[i])
        j = i - DEPTH // 2
        if 0 <= j < len(blocks):
            held_back[j] = second(*blocks[j], *made.pop(j))
        k = i - DEPTH
        if 0 <= k < len(blocks):
            third(*blocks[k], *held_back.pop(k))


def late_kernel(n, heads, *refs):
    rest = by_slot(REST_ORDER, refs[:n])
    kv_late, qg_early, qg_late, kv_early, dq, dkv, turned = refs[n:]
    place_all(rest, qg_late, kv_early, group_index())
    total = dkv.shape[1]
    qg, kv = (qg_early, qg_late), (kv_early, kv_late)
    blocks = [(h, start) for h in range(heads) for start in range(0, total - WINDOW, TILE)]
    lanes_of = [slice(h * HEAD_DIM, (h + 1) * HEAD_DIM) for h in range(heads)]
    key_ts = [load(kv, 0, 0, total, lanes).T for lanes in lanes_of]
    for h in range(heads):
        turned[h] = key_ts[h][:, :WINDOW]

    def products(h, start):
        qb, gb = (load(qg, t, start + WINDOW, start + WINDOW + TILE, lanes_of[h]) for t in range(2))
        kb, vb = (load(kv, t, start, start + 3 * TILE, lanes_of[h]) for t in range(2))
        return dot(kb, qb, NT), dot(vb, gb, NT)

    def gradients(h, start, p_low, ds):
        lanes = lanes_of[h]
        keys = slice(start, start + 3 * TILE)
        mine = slice(start + WINDOW, start + WINDOW + TILE)
        qb, gb = (load(qg, t, start + WINDOW, start + WINDOW + TILE, lanes) for t in range(2))
        dq[slice(start, start + TILE), lanes] = (
            (dot(key_ts[h][:, keys], ds, NN) * SCALE).astype(jnp.bfloat16).T
        )
        for t, add in enumerate((dot(ds, qb, NN), dot(p_low, gb, NN))):
            if start == 0:
                dkv[t, keys, lanes] = add
            else:
                older = slice(start, start + 2 * TILE)
                dkv[t, older, lanes] += add[: 2 * TILE]
                dkv[t, mine, lanes] = add[2 * TILE :]

    staged(blocks, products, lambda h, start, s, dp: softmax_block(s, dp, 0.0, 0)[:2], gradients)


def early_kernel(n, heads, *refs):
    qg_early, qg_late, kv_early, kv_late, kv_halo, dq_in, dkv_in, turned = refs[:8]
    refs = refs[8:]
    dq_out = refs[: n // 2]
    front, stat, dq, acc = refs[n // 2 :]
    me = group_index()
    rows = dq_out[0].shape[1]
    first = lax.axis_index("chunk") == 0
    stat[...] = jnp.zeros_like(stat)
    dq[WINDOW:] = dq_in[...]
    acc[...] = dkv_in[:, :WINDOW]
    bias = jnp.where(first, MASKED, 0.0)
    qg, kv = (qg_early, qg_late), (kv_halo, kv_early, kv_late)
    blocks = [(h, start) for h in range(heads) for start in range(0, WINDOW, TILE)]
    lanes_of = [slice(h * HEAD_DIM, (h + 1) * HEAD_DIM) for h in range(heads)]
    key_ts = [
        jnp.concatenate([kv_halo[0, :, lanes].T, turned[h]], axis=1)
        for h, lanes in enumerate(lanes_of)
    ]

    def products(h, start):
        qb, gb = (load(qg, t, start, start + TILE, lanes_of[h]) for t in range(2))
        kb, vb = (load(kv, t, start, start + 3 * TILE, lanes_of[h]) for t in range(2))
        return dot(kb, qb, NT), dot(vb, gb, NT)

    def probabilities(h, start, s, dp):
        p_low, ds, stats = softmax_block(s, dp, bias, WINDOW - start)
        for c, rows_of in enumerate(stats):
            at = slice(start + c * HALF, start + (c + 1) * HALF)
            for k, value in enumerate(rows_of):
                stat[3 * h + k : 3 * h + k + 1, at] = value
        return p_low, ds

    def gradients(h, start, p_low, ds):
        lanes = lanes_of[h]
        keys = slice(start, start + 3 * TILE)
        qb, gb = (load(qg, t, start, start + TILE, lanes) for t in range(2))
        dq[slice(start, start + TILE), lanes] = (
            (dot(key_ts[h][:, keys], ds, NN) * SCALE).astype(jnp.bfloat16).T
        )
        own = slice(0, start + TILE)
        acc[0, own, lanes] += dot(ds[WINDOW - start :], qb, NN)
        acc[1, own, lanes] += dot(p_low[WINDOW - start :], gb, NN)

    staged(blocks, products, probabilities, gradients)
    for m in range(n):
        dq_out[m // 2][m % 2] = dq[pl.ds(aligned(jnp.bitwise_xor(me, m), rows), rows)]
    front[0] = (acc[0] * SCALE).astype(jnp.bfloat16)
    front[1] = acc[1].astype(jnp.bfloat16)


def edge_kernel(n, heads, *refs):
    kv_early, kv_late, qg, front, dkv_in, stat = refs[:6]
    refs = refs[6:]
    out = refs[:n]
    full, acc = refs[n:]
    me = group_index()
    total = dkv_in.shape[1]
    done = total - WINDOW
    rows = total // n
    kv = (kv_early, kv_late)
    row = lax.broadcasted_iota(jnp.int32, (TILE, TILE), 0)
    col = lax.broadcasted_iota(jnp.int32, (TILE, TILE), 1)
    acc[...] = dkv_in[:, WINDOW:]
    blocks = [(h, start) for h in range(heads) for start in range(0, WINDOW, TILE)]
    lanes_of = [slice(h * HEAD_DIM, (h + 1) * HEAD_DIM) for h in range(heads)]

    def products(h, start):
        mine = slice(start, start + TILE)
        kb, vb = (load(kv, t, done + start, total, lanes_of[h]) for t in range(2))
        return dot(kb, qg[0, mine, lanes_of[h]], NT), dot(vb, qg[1, mine, lanes_of[h]], NT)

    def probabilities(h, start, s, dp):
        mine = slice(start, start + TILE)
        newest = jnp.where(row > col, s[:TILE], MASKED)
        s = newest if len(s) == TILE else jnp.concatenate([newest, s[TILE:]], axis=0)
        top, inverse, dots = (stat[3 * h + k : 3 * h + k + 1, mine] for k in range(3))
        p = jnp.exp2(s * SCALE_LOG2 - top) * inverse
        return p.astype(jnp.bfloat16), (p * (dp - dots)).astype(jnp.bfloat16)

    def gradients(h, start, p_low, ds):
        mine = slice(start, start + TILE)
        at = slice(done - WINDOW + start, done)
        acc[0, at, lanes_of[h]] += dot(ds, qg[0, mine, lanes_of[h]], NN)
        acc[1, at, lanes_of[h]] += dot(p_low, qg[1, mine, lanes_of[h]], NN)

    staged(blocks, products, probabilities, gradients)
    full[:, :WINDOW] = front[...]
    full[0, WINDOW:] = (acc[0] * SCALE).astype(jnp.bfloat16)
    full[1, WINDOW:] = acc[1].astype(jnp.bfloat16)
    for m in range(n):
        out[m][...] = full[:, pl.ds(aligned(jnp.bitwise_xor(me, m), rows), rows)]


def core_kernel(*refs):
    *pieces, out = refs
    for slot, piece in enumerate(by_slot(DQ_ORDER, pieces)):
        out[slot] = piece[1]


def unpack_kernel(n, *refs):
    chips = n // 2
    dq_in = by_slot(DQ_ORDER, refs[:chips])
    other = refs[chips]
    dkv_in = by_slot(DKV_ORDER, refs[chips + 1 : chips + 1 + n])
    dq, dk, dv, sems = refs[chips + 1 + n :]
    me = group_index()
    width = other.shape[2]
    pairs = []
    for m in range(n):
        cols = pl.ds(aligned(jnp.bitwise_xor(me, m), width), width)
        pairs.append((other.at[m // 2] if m % 2 else dq_in[m // 2].at[0], dq.at[:, cols]))
        pairs.append((dkv_in[m].at[0], dk.at[:, cols]))
        pairs.append((dkv_in[m].at[1], dv.at[:, cols]))
    copy_all(pairs, sems)


def call(kernel, outs, scratch, sems, *operands, space=pl.ANY, limit=VMEM_LIMIT, flops=0):
    held = pl.BlockSpec(memory_space=pltpu.VMEM)
    loose = pl.BlockSpec(memory_space=space)
    arrays = [x[0] if isinstance(x, tuple) else x for x in operands]
    return pl.pallas_call(
        kernel,
        out_shape=outs,
        in_specs=[held if isinstance(x, tuple) else loose for x in operands],
        out_specs=[held if not isinstance(x, jax.ShapeDtypeStruct) else pl.BlockSpec(memory_space=pl.ANY) for x in outs],
        scratch_shapes=[*scratch, *([pltpu.SemaphoreType.DMA((sems,))] if sems else [])],
        compiler_params=pltpu.CompilerParams(vmem_limit_bytes=limit),
        cost_estimate=pl.CostEstimate(flops=flops, bytes_accessed=0, transcendentals=0) if flops else None,
    )(*arrays)


def held(arrays):
    return [(x,) for x in arrays]


def vmem(shape):
    return pltpu.VMEM(shape.shape, shape.dtype)


def order_of(order, n):
    return [m for m in order if m < n] + list(range(len(order), n))


def by_slot(order, refs):
    order = order_of(order, len(refs))
    return [refs[order.index(m)] for m in range(len(refs))]


def exchanged(order, pieces, step=1):
    n = len(pieces)
    return [
        lax.ppermute(pieces[m], GROUP, [(i, i ^ (step * m)) for i in range(step * n)]) if m else pieces[0]
        for m in order_of(order, n)
    ]


def per_device(queries, key_vectors, value_vectors, grad_output):
    n = group_size()
    chunks = lax.axis_size("chunk")
    rows, model = queries.shape
    heads = HEADS // n
    width = model // n
    total = n * rows
    done = total - WINDOW
    piece = bf16(2, rows, width)
    arguments = (queries, grad_output, key_vectors, value_vectors)

    def packed(late_pair, early_pair):
        return call(
            functools.partial(pack_kernel, n, late_pair, early_pair), [vmem(piece)] * n,
            [vmem(bf16(2, rows, model))], 2, *arguments, space=pltpu.HBM, limit=None,
        )

    crit = exchanged(CRIT_ORDER, packed((2, 3), (0, 1)))
    half = total // 2
    end = vmem(bf16(2, WINDOW, width))
    halves = vmem(bf16(2, half, width))
    sends = call(
        functools.partial(halo_kernel, n),
        [halves, halves] + [end, end] * (half > WINDOW), [], 0, *held(crit),
    )
    kv_late, qg_early = sends[:2]
    kv_send, qg_send = sends[-2:]
    forward = [(i, i + 1) for i in range(chunks - 1)]
    backward = [(i + 1, i) for i in range(chunks - 1)]
    kv_halo = lax.ppermute(kv_send, "chunk", forward)
    qg_halo = lax.ppermute(qg_send, "chunk", backward)
    rest = exchanged(REST_ORDER, packed((0, 1), (2, 3)))
    stat_out = vmem(f32(-(-3 * heads // 8) * 8, WINDOW))
    qg_late, kv_early, dq_late, partial, turned = call(
        functools.partial(late_kernel, n, heads),
        [
            halves, halves, vmem(bf16(done, width)), vmem(f32(2, total, width)),
            vmem(bf16(heads, HEAD_DIM, WINDOW)),
        ],
        [], 0,
        *held(rest), (kv_late,), (qg_early,), flops=LATE_FLOPS,
    )
    *dq, front, stat = call(
        functools.partial(early_kernel, n, heads),
        [vmem(bf16(2, rows, width))] * (n // 2) + [end, stat_out],
        [vmem(bf16(total, width)), vmem(f32(2, WINDOW, width))], 0,
        *held((qg_early, qg_late, kv_early, kv_late, kv_halo, dq_late, partial, turned)),
    )
    stat_halo = lax.ppermute(stat, "chunk", backward)
    dq = exchanged(DQ_ORDER, dq, 2)
    other, = call(
        core_kernel, [vmem(bf16(n // 2, rows, width))], [], 0, *held(dq)
    )
    other = lax.ppermute(other, GROUP, [(i, i ^ 1) for i in range(n)])
    dkv = call(
        functools.partial(edge_kernel, n, heads),
        [vmem(piece)] * n, [vmem(bf16(2, total, width)), vmem(f32(2, done, width))], 0,
        *held((kv_early, kv_late, qg_halo, front, partial, stat_halo)), flops=EDGE_FLOPS,
    )
    dkv = exchanged(DKV_ORDER, dkv)
    out = bf16(rows, model)
    return tuple(
        call(functools.partial(unpack_kernel, n), [out] * 3, [], 3 * n, *held(dq), (other,), *held(dkv))
    )


def solution(mesh):
    seq, head = mesh.devices.shape
    part = max(1, min(seq, HEADS // 2 // head))
    fine = Mesh(mesh.devices.reshape(seq // part, part, head), AXES)
    placed = P(AXES, None)
    return jax.shard_map(
        per_device,
        mesh=fine,
        in_specs=(placed,) * 4,
        out_specs=(placed,) * 3,
        check_vma=False,
    )
```
